32 devices in a mesh: dp: 16 (over z, y, x), section: 2 (over core).
Axes of the slice: x: 2, y: 2, z: 4, core: 2. Of those that a mesh axis runs over, the one named last changes fastest.
Arguments:
- hidden_in: bfloat16 [4096, 1024], P('dp'), may hold values from -6 to 6
- seq_lengths: int32 [16, 6], P('dp'), may hold values from 1 to 128, 256 in all within a row
- norm_gain: float32 [2, 1024], P('section'), may hold values from 0.5 to 1.5
- in_proj: bfloat16 [2, 1024, 4096], P('section'), may hold values from -0.1875 to 0.1875
- conv_weight: float32 [2, 4, 2048], P('section'), may hold values from -3 to 3
- conv_bias: float32 [2, 2048], P('section'), may hold values from -3 to 3
- select_proj: bfloat16 [2, 96, 2048], P('section'), may hold values from -0.125 to 0.125
- step_proj: bfloat16 [2, 64, 2048], P('section'), may hold values from -0.75 to 0.75
- step_bias: float32 [2, 2048], P('section'), may hold values from -6.9 to -2.3
- decay_log: float32 [2, 16, 2048], P('section'), may hold values from 0 to 2.77
- skip_gain: float32 [2, 2048], P('section'), may hold values from 0.5 to 1.5
- out_proj: bfloat16 [2, 2048, 1024], P('section'), may hold values from -0.25 to 0.25
- cotangent: bfloat16 [4096, 1024], P('dp'), may hold values from -6 to 6
Outputs:
- activations: float32 [2, 4096, 1024], P('section', 'dp')
- input_grads: float32 [2, 4096, 1024], P('section', 'dp')
- grad_norm_gain: float32 [2, 1024], P('section')
- grad_in_proj: float32 [2, 1024, 4096], P('section')
- grad_conv_weight: float32 [2, 4, 2048], P('section')
- grad_conv_bias: float32 [2, 2048], P('section')
- grad_select_proj: float32 [2, 96, 2048], P('section')
- grad_step_proj: float32 [2, 64, 2048], P('section')
- grad_step_bias: float32 [2, 2048], P('section')
- grad_decay_log: float32 [2, 16, 2048], P('section')
- grad_skip_gain: float32 [2, 2048], P('section')
- grad_out_proj: float32 [2, 2048, 1024], P('section')
The draws below stay inside these ranges and needn't reach their ends.
Inputs may be any that keep to these rules, and one draw needn't show every extreme that they name: Each row of seq_lengths sums to 256; the largest entry of every row is exactly 128.
All inputs are finite; a program needn't handle non-finite values.
Results may differ from the reference program's by a relative error of at most 0.012.
The reference program's roundings to bfloat16 on the way count: a program that leaves them out, or rounds other values in their place, can miss the bound.
Values may be sent and summed in bfloat16 or wider, within the bound.
No kernel may reach another device: no remote copies, remote signals or barrier semaphores. Data moves between devices by JAX's collectives and lax.ppermute only.
A program may use at most 128 MiB of HBM per device.

```python
import math
import jax
import jax.numpy as jnp
import numpy as np
from jax import lax

D = 1024
INNER = 2048
STATE = 16
RANK = 64
CONV = 4
XW = 96
TOK_DEV = 256
SEQ_DEV = 6
SEQ_MOST = 128
LAYERS = 2
CLUSTERS = 16
TOKENS = 4096


def level_of(stream_key, shape, cuts, smallest, top_value):
    loudness = 1.0
    for dim, blocks in cuts:
        heights = jax.random.uniform(jax.random.fold_in(jax.random.fold_in(stream_key, 6), dim), (blocks,), jnp.float32, smallest / len(cuts), top_value / len(cuts))
        loudness = loudness * jnp.repeat(jnp.exp(heights), shape[dim] // blocks).reshape((-1,) + (1,) * (len(shape) - 1 - dim))
    return loudness


def profile(number_of, total, reach, slope):
    portions = [(1 << 20) // math.isqrt(rank ** slope) + 1 for rank in range(2, number_of + 1)]
    spare, given = total - reach - (number_of - 1), [1] * (number_of - 1)
    while spare > 0:
        candidates = [i for i in range(number_of - 1) if given[i] < reach]
        pool, remaining = sum([portions[i] for i in candidates]), spare
        for i in candidates:
            extra = min(reach - given[i], max(1, remaining * portions[i] // pool), spare)
            given[i] = given[i] + extra
            spare = spare - extra
    return np.array([reach] + given)


def uneven_parts(rng, amount, total, bound, slope):
    if amount == 2:
        one = jax.random.randint(rng, (), max(1, total - bound), min(bound, total - 1) + 1)
        return jnp.stack([one, total - one])
    sizes = jnp.asarray(profile(amount, total, bound, slope), jnp.int32)
    twos = (amount - 1) // 2
    giver, sink = sizes[1:1 + 2 * twos:2], sizes[2:2 + 2 * twos:2]
    room = jnp.minimum(giver - 1, bound - sink)
    moved = jax.random.randint(jax.random.fold_in(rng, 1), (twos,), 0, 1 << 20) % (room + 1)
    sizes = sizes.at[1:1 + 2 * twos:2].set(giver - moved).at[2:2 + 2 * twos:2].set(sink + moved)
    return sizes[jax.random.permutation(jax.random.fold_in(rng, 2), amount)]


def noise(own_key, shape, deviation, bound, split=(), held_as=jnp.bfloat16):
    drawn = jax.random.normal(own_key, shape, jnp.float32) * deviation
    if len(split) > 0:
        drawn = level_of(own_key, shape, split, -0.22, 0.18) * drawn
    return jnp.clip(drawn, min=-bound, max=bound).astype(held_as)


def setup_inputs(seed: int = 0) -> dict:
    splits = jax.random.split(jax.random.key(seed), 14)
    return {
        "hidden_in": noise(splits[0], (TOKENS, D), 1.0, 6.0, ((0, 16),)),
        "seq_lengths": jax.vmap(lambda own: uneven_parts(own, SEQ_DEV, TOK_DEV, SEQ_MOST, 2))(jax.random.split(splits[1], CLUSTERS)).reshape((CLUSTERS, SEQ_DEV)).astype(jnp.int32),
        "norm_gain": jnp.clip(0.5 + 1.0 * jax.random.uniform(splits[2], (LAYERS, D), jnp.float32) ** level_of(splits[2], (LAYERS, D), ((0, 2),), -0.2, 0.2), 0.5, 1.5),
        "in_proj": noise(splits[3], (LAYERS, D, 2 * INNER), D ** -0.5, 0.1875, ((0, 2),)),
        "conv_weight": noise(splits[4], (LAYERS, CONV, INNER), CONV ** -0.5, 3.0, ((0, 2),), jnp.float32),
        "conv_bias": noise(splits[5], (LAYERS, INNER), 0.5, 3.0, ((0, 2),), jnp.float32),
        "select_proj": noise(splits[6], (LAYERS, XW, INNER), INNER ** -0.5, 0.125, ((0, 2),)),
        "step_proj": noise(splits[7], (LAYERS, RANK, INNER), RANK ** -0.5, 0.75, ((0, 2),)),
        "step_bias": jnp.clip(-6.9 + 4.6000001430511475 * jax.random.uniform(splits[8], (LAYERS, INNER), jnp.float32) ** level_of(splits[8], (LAYERS, INNER), ((0, 2),), -0.2, 0.2), -6.9, -2.3),
        "decay_log": jnp.clip(2.77 * jax.random.uniform(splits[9], (LAYERS, STATE, INNER), jnp.float32) ** level_of(splits[9], (LAYERS, STATE, INNER), ((0, 2),), -0.2, 0.2), 0.0, 2.77),
        "skip_gain": jnp.clip(0.5 + 1.0 * jax.random.uniform(splits[10], (LAYERS, INNER), jnp.float32) ** level_of(splits[10], (LAYERS, INNER), ((0, 2),), -0.2, 0.2), 0.5, 1.5),
        "out_proj": noise(splits[11], (LAYERS, INNER, D), (INNER // 4) ** -0.5, 0.25, ((0, 2),)),
        "cotangent": noise(splits[12], (TOKENS, D), 1.0, 6.0, ((0, 16),)),
    }


@jax.custom_vjp
def low(v):
    return lax.optimization_barrier(v.astype(jnp.bfloat16)).astype(jnp.float32)

@jax.custom_vjp
def low_back(v):
    return v

def low_keep(v):
    return (low(v), None)

def low_pass(kept, grad):
    return (grad,)

def back_keep(v):
    return (v, None)

def back_low(kept, grad):
    return (low(grad),)
low.defvjp(low_keep, low_pass)
low_back.defvjp(back_keep, back_low)
EPS = 1e-05
HIGHEST = lax.Precision.HIGHEST

def project(values, weight):
    return low_back(jnp.dot(low(values), weight, precision=HIGHEST, preferred_element_type=jnp.float32))

def place_tokens(index, begins):
    hits = index[..., :, None] >= begins[..., None, :]
    begin = lax.optimization_barrier(jnp.max(jnp.where(hits, begins[..., None, :], 0), axis=-1))
    position = index - begin
    return (position, (position == 0).astype(jnp.float32))

def selective_scan(step_size, conv_out, input_map, output_map, keep, decay_rate):
    clusters, length = keep.shape
    block = math.gcd(length, 64)

    def blocked(value):
        moved = jnp.moveaxis(value, 1, 0)
        return moved.reshape((length // block, block) + moved.shape[1:])

    def advance(carried, item):
        step_t, conv_t, in_t, out_t, keep_t = item
        carried = jnp.exp(step_t[:, None, :] * decay_rate) * carried * keep_t[:, None, None] + in_t[:, :, None] * (step_t * conv_t)[:, None, :]
        return (carried, lax.optimization_barrier(jnp.sum(out_t[:, :, None] * carried, axis=1)))

    def run_block(carried, items):
        return lax.scan(advance, carried, items)
    start_state = jnp.zeros((clusters, decay_rate.shape[0], decay_rate.shape[1]), jnp.float32)
    items = tuple((blocked(value) for value in (step_size, conv_out, input_map, output_map, keep)))
    _, outs = lax.scan(jax.checkpoint(run_block), start_state, items)
    return jnp.moveaxis(outs.reshape((length,) + outs.shape[2:]), 0, 1)

def mamba_layer(weights, rows, position, resets):
    norm_scale, in_weight, conv_kernel, conv_shift, select_weight, step_weight, step_shift, log_decay, skip_scale, out_weight = weights
    length = rows.shape[1]
    inner_width = conv_shift.shape[0]
    kernel_taps = conv_kernel.shape[0]
    low_rank = step_weight.shape[0]
    state_count = log_decay.shape[0]
    mean_sq = lax.optimization_barrier(jnp.mean(rows * rows, axis=-1, keepdims=True))
    normed = rows * lax.rsqrt(mean_sq + EPS) * norm_scale
    both = project(normed, in_weight)
    inner_in = both[..., :inner_width]
    gate_in = both[..., inner_width:]
    padded = jnp.pad(inner_in, ((0, 0), (kernel_taps - 1, 0), (0, 0)))
    mixed = conv_shift
    for delay in range(kernel_taps):
        start = kernel_taps - 1 - delay
        mixed = mixed + conv_kernel[start] * padded[:, start:start + length] * (position >= delay).astype(jnp.float32)[..., None]
    conv_out = jax.nn.silu(mixed)
    selected = project(conv_out, select_weight.T)
    step_size = jax.nn.softplus(project(selected[..., :low_rank], step_weight) + step_shift)
    input_map = selected[..., low_rank:low_rank + state_count]
    output_map = selected[..., low_rank + state_count:]
    decay_rate = -jnp.exp(log_decay)
    scanned = selective_scan(step_size, conv_out, input_map, output_map, 1.0 - resets, decay_rate)
    gated = (scanned + skip_scale * conv_out) * jax.nn.silu(gate_in)
    return rows + project(gated, out_weight)

def reference(hidden_in, seq_lengths, norm_gain, in_proj, conv_weight, conv_bias, select_proj, step_proj, step_bias, decay_log, skip_gain, out_proj, cotangent):
    clusters = seq_lengths.shape[0]
    width = hidden_in.shape[1]
    length = hidden_in.shape[0] // clusters
    ends = jnp.cumsum(seq_lengths, axis=1, dtype=jnp.int32)
    begins = ends - seq_lengths
    index = jnp.broadcast_to(jnp.arange(length, dtype=jnp.int32)[None, :], (clusters, length))
    position, resets = place_tokens(index, begins)
    weights = tuple((item.astype(jnp.float32) for item in (norm_gain, in_proj, conv_weight, conv_bias, select_proj, step_proj, step_bias, decay_log, skip_gain, out_proj)))
    layers = norm_gain.shape[0]
    rows = hidden_in.astype(jnp.float32).reshape(clusters, length, width)
    bumps = jnp.zeros((layers - 1, clusters, length, width), jnp.float32)

    def forward(weights, rows, bumps):
        outputs = []
        current = rows
        for layer in range(layers):
            if layer > 0:
                current = low_back(low(current)) + bumps[layer - 1]
            current = mamba_layer(tuple((item[layer] for item in weights)), current, position, resets)
            outputs.append(current)
        return (current, jnp.stack(outputs))
    final, pullback, stacked = jax.vjp(forward, weights, rows, bumps, has_aux=True)
    grad_weights, grad_rows, grad_bumps = pullback(cotangent.astype(jnp.float32).reshape(clusters, length, width))
    activations = stacked.reshape(layers, clusters * length, width)
    input_grads = jnp.concatenate([grad_rows[None], grad_bumps], axis=0).reshape(layers, clusters * length, width)
    return (activations, input_grads, grad_weights[0], grad_weights[1], grad_weights[2], grad_weights[3], grad_weights[4], grad_weights[5], grad_weights[6], grad_weights[7], grad_weights[8], grad_weights[9])
```

```python
from functools import partial
import math

import jax
import jax.numpy as jnp
from jax import lax
from jax.experimental import pallas as pl
from jax.experimental.pallas import tpu as pltpu
from jax.sharding import PartitionSpec as P

EPS = 1e-05
LN2 = math.log(2.0)
FOREVER = 1e30
TB = 16
CB = 512
GATE_CHUNK = 32
CHUNK = 128
WIDE_CHUNK = 256
F32 = jnp.float32
LITTLE = pl.CostEstimate(flops=10**6, bytes_accessed=10**4, transcendentals=0)
BF16 = jnp.bfloat16
PLANE = 4
VMEM_LIMIT = 60 * 1024 * 1024


def mm(a, b):
    return jnp.dot(a, b, preferred_element_type=F32)


def mm_nt(a, b):
    return lax.dot_general(a, b, (((1,), (1,)), ((), ())), preferred_element_type=F32)


def mm_tn(a, b):
    return lax.dot_general(a, b, (((0,), (0,)), ((), ())), preferred_element_type=F32)


def iota(shape, dim):
    return lax.broadcasted_iota(jnp.int32, shape, dim)


def split_hi_lo(value):
    hi = value.astype(BF16)
    return hi, (value - hi.astype(F32)).astype(BF16)


def softplus(value):
    small = jnp.exp(-jnp.abs(value))
    series = small * (1.0 - small * (0.5 - small * (1.0 / 3.0 - 0.25 * small)))
    return jnp.maximum(value, 0.0) + jnp.where(small < 2.0**-6, series, jnp.log(1.0 + small))


def places(lengths, rows, lanes):
    index = iota((rows, lanes), 0)
    begin = jnp.zeros((rows, lanes), jnp.int32)
    start = jnp.int32(0)
    for number in range(lengths.shape[1]):
        begin = jnp.where(index >= start, start, begin)
        start = start + lengths[0, number]
    return index - begin


def fold8(value):
    total = value[:8]
    for start in range(8, value.shape[0], 8):
        total = total + value[start : start + 8]
    return total


def spread_diagonal(columns, states, diag):
    count = columns.shape[0]
    wide = TB * states
    expand = (iota((states, wide), 1) % states == iota((states, wide), 0)).astype(BF16)
    own = iota((count, wide), 0) % TB == iota((count, wide), 1) // states
    for part, piece in enumerate(split_hi_lo(columns)):
        spread = jnp.where(own, mm(piece, expand), 0.0).astype(BF16)
        for block in range(count // TB):
            diag[block, part * TB : (part + 1) * TB, :] = spread[block * TB : (block + 1) * TB]


def spread_lanes(turned, states, wide):
    for token in range(turned.shape[1]):
        wide[token * states : (token + 1) * states, :] = jnp.broadcast_to(
            turned[:, token : token + 1], (states, wide.shape[1])
        )


def repeat_lanes(value, times):
    return jnp.concatenate([value] * times, axis=1)


def conv_taps(window, position, delays):
    taps = []
    for delay in range(delays):
        moved = window[8 - delay : 8 - delay + position.shape[0]]
        taps.append(moved if delay == 0 else jnp.where(position >= delay, moved, 0.0))
    return taps


def conv_value(taps, weight, bias):
    value = jnp.broadcast_to(bias, taps[0].shape)
    last = len(taps) - 1
    for delay, tap in enumerate(taps):
        value = value + weight[last - delay : last - delay + 1] * tap
    return value


def forward_kernel(
    number,
    aliased,
    lengths,
    ids,
    rows_ref,
    gain_ref,
    in_hbm,
    cw_ref,
    cbias_ref,
    sel_ref,
    step_ref,
    sbias_ref,
    dlog_ref,
    skip_ref,
    out_hbm,
    *rest,
):
    made = 12
    rest = rest[made if aliased else 0 :]
    out_hbm2, outb_hbm, selt_hbm, selo_hbm, *kept = rest[:10]
    s_hbm, factors = rest[10:12]
    rest = rest[12:]
    (
        result_v,
        low_v,
        selt_ref,
        selo_ref,
        sig_ref,
        turn_v,
        xi_ref,
        z_ref,
        y_ref,
        delta_ref,
        xc_v,
        in_v,
        out_v,
        s0_v,
        s1_v,
        u_v,
        xcb_v,
        dp_v,
        dx_v,
        pos_v,
        bb_v,
        cd_v,
        gb_v,
        in_sem,
        out_sem,
        s_sem,
        send_sem,
        keep_sem,
        last_sem,
    ) = rest
    count, width = rows_ref.shape
    inner = cbias_ref.shape[1]
    blocks = inner // CB
    states = dlog_ref.shape[0]
    rank = step_ref.shape[0]
    taps = cw_ref.shape[0]

    def body():
        started = []

        def keep(item, k):
            source = (xi_ref, z_ref, y_ref, delta_ref, sig_ref, xc_v)[item]
            copy = pltpu.make_async_copy(source.at[k], kept[item].at[k], keep_sem.at[item, k])
            copy.start()
            started.append(copy)

        in_copies = [
            pltpu.make_async_copy(in_hbm.at[:, pl.ds(k * CB, CB)], in_v.at[k], in_sem.at[k])
            for k in range(2 * blocks)
        ]
        out_copy = pltpu.make_async_copy(out_hbm, out_v, out_sem)
        for copy in in_copies:
            copy.start()
        out_copy.start()
        pos_v[...] = places(lengths, count, CB)

        def norm(step, _):
            at = pl.ds(pl.multiple_of(step * WIDE_CHUNK, WIDE_CHUNK), WIDE_CHUNK)
            a = rows_ref[at, :].astype(F32)
            scale = lax.rsqrt(jnp.mean(a * a, axis=-1, keepdims=True) + EPS)
            u_v[at, :] = (a * scale * gain_ref[...]).astype(BF16)
            return 0

        lax.fori_loop(0, count // WIDE_CHUNK, norm, 0)
        sel = jnp.zeros((count, sel_ref.shape[0]), F32)
        selt = jnp.zeros((sel_ref.shape[0], count), F32)
        for k in range(blocks):
            cols = slice(k * CB, (k + 1) * CB)
            in_copies[k].wait()
            xi_ref[k, 0:8, :] = jnp.zeros((8, CB), F32)
            xi_ref[k, 8:, :] = mm(u_v[...], in_v[k])

            def conv(step, _, k=k, cols=cols):
                start = pl.multiple_of(step * WIDE_CHUNK, WIDE_CHUNK)
                at = pl.ds(start, WIDE_CHUNK)
                window = xi_ref[k, pl.ds(start, WIDE_CHUNK + 8), :]
                value = conv_value(
                    conv_taps(window, pos_v[at, :], taps), cw_ref[:, cols], cbias_ref[:, cols]
                )
                xc = value * jax.nn.sigmoid(value)
                xc_v[k, at, :] = xc
                xcb_v[k, at, :] = xc.astype(BF16)
                return 0

            lax.fori_loop(0, count // WIDE_CHUNK, conv, 0)
            keep(0, k)
            keep(5, k)
            sel = sel + mm_nt(xcb_v[k], sel_ref[:, cols])
            selt = selt + mm_nt(sel_ref[:, cols], xcb_v[k])
        selo_ref[...] = sel
        selt_ref[...] = selt
        dlb = sel[:, :rank].astype(BF16)
        spread_lanes(selt_ref[rank : rank + states, :], states, bb_v)
        spread_diagonal(selo_ref[:, rank + states : rank + 2 * states], states, cd_v)
        for k in range(blocks):
            cols = slice(k * CB, (k + 1) * CB)
            delta_ref[k] = mm(dlb, step_ref[:, cols]) + sbias_ref[:, cols]

            def soften(step, _, k=k):
                at = pl.ds(pl.multiple_of(step * WIDE_CHUNK, WIDE_CHUNK), WIDE_CHUNK)
                q = delta_ref[k, at, :]
                delta = softplus(q)
                delta_ref[k, at, :] = delta
                sig_ref[k, at, :] = jax.nn.sigmoid(q)
                dp_v[k, at, :] = jnp.where(pos_v[at, :] == 0, FOREVER, delta)
                dx_v[k, at, :] = delta * xc_v[k, at, :]
                return 0

            lax.fori_loop(0, count // WIDE_CHUNK, soften, 0)
            keep(3, k)
            keep(4, k)
        for k in range(blocks):
            in_copies[blocks + k].wait()
            z_ref[k] = mm(u_v[...], in_v[blocks + k])

        s_v = (s0_v, s1_v)
        wide = TB * states

        def s_copy(k, slot):
            return pltpu.make_async_copy(s_v[slot], s_hbm.at[k], s_sem.at[slot])

        def read_out(k, block):
            start = pl.multiple_of(block * TB, TB)
            span = pl.ds(pl.multiple_of(start * states, wide), wide)
            both = mm(cd_v[block], s_v[k % 2][span, :])
            y_ref[k, pl.ds(start, TB), :] = both[:TB] + both[TB:]

        for k in range(blocks):
            cols = slice(k * CB, (k + 1) * CB)
            slot = k % 2
            if k >= 2:
                s_copy(k - 2, slot).wait()
            rate = -jnp.exp(dlog_ref[:, cols]) * (1.0 / LN2)

            def scan(block, state, k=k, slot=slot, rate=rate):
                start = pl.multiple_of(block * TB, TB)
                if k > 0:
                    read_out(k - 1, block)
                for token in range(TB):
                    if token % 8 == 0:
                        at = pl.ds(pl.multiple_of(start + token, 8), 8)
                        steps, drives = dp_v[k, at, :], dx_v[k, at, :]
                    row = slice(token % 8, token % 8 + 1)
                    here = pl.ds(pl.multiple_of((start + token) * states, states), states)
                    decay = jnp.exp2(steps[row] * rate)
                    state = decay * state + repeat_lanes(bb_v[here, :], CB // 128) * drives[row]
                    s_v[slot][here, :] = state.astype(BF16)
                return state

            lax.fori_loop(0, count // TB, scan, jnp.zeros((states, CB), F32))
            s_copy(k, slot).start()
        for block in range(count // TB):
            read_out(blocks - 1, block)
        for k in range(blocks):
            cols = slice(k * CB, (k + 1) * CB)

            def gate(step, _, k=k, cols=cols):
                at = pl.ds(pl.multiple_of(step * WIDE_CHUNK, WIDE_CHUNK), WIDE_CHUNK)
                z = z_ref[k, at, :]
                full = y_ref[k, at, :] + skip_ref[:, cols] * xc_v[k, at, :]
                sz = jax.nn.sigmoid(z)
                gated = z * sz
                gb_v[k, at, :] = (full * gated).astype(BF16)
                z_ref[k, at, :] = gated
                y_ref[k, at, :] = full * (sz * (1.0 + z * (1.0 - sz)))
                return 0

            lax.fori_loop(0, count // WIDE_CHUNK, gate, 0)
            keep(1, k)
            keep(2, k)
        copies = started
        for start in range(0, width, CB):
            turn_v[start : start + CB, :] = u_v[:, start : start + CB].astype(F32).T.astype(BF16)
        for k in range(blocks):
            turn_v[width + k * CB : width + (k + 1) * CB, :] = gb_v[k].astype(F32).T.astype(BF16)
        last = [(turn_v, factors), (selt_ref, selt_hbm), (selo_ref, selo_hbm)]
        out_copy.wait()
        result = rows_ref[...].astype(F32)
        for k in range(blocks):
            result = result + mm(gb_v[k], out_v[k * CB : (k + 1) * CB, :])
        result_v[...] = result
        low_v[...] = result.astype(BF16)
        last += [(low_v, outb_hbm), (result_v, out_hbm2)]
        last = [
            pltpu.make_async_copy(source, target, last_sem.at[item]) for item, (source, target) in enumerate(last)
        ]
        for copy in last:
            copy.start()
        for k in range(max(0, blocks - 2), blocks):
            s_copy(k, k % 2).wait()
        for copy in copies + last:
            copy.wait()

    pl.when(ids[0] == number)(body)


def vmem():
    return pl.BlockSpec(memory_space=pltpu.VMEM)


def smem():
    return pl.BlockSpec(memory_space=pltpu.SMEM)


def hbm():
    return pl.BlockSpec(memory_space=pl.ANY)


def forward(number, lengths, ids, rows, weights, earlier):
    gain, in_w, conv_w, conv_b, sel_w, step_w, step_b, dlog, skip, out_w = weights
    count, width = rows.shape
    inner = conv_b.shape[1]
    blocks = inner // CB
    states = dlog.shape[0]
    picks = sel_w.shape[0]
    cube = (blocks, count, CB)
    tall = (blocks, count + 8, CB)
    kept = [(tall, F32)] + [(cube, F32)] * 5
    made = [((count, width), F32), ((count, width), BF16), ((picks, count), F32), ((count, picks), F32)]
    factors = ((width + inner, count), BF16)
    out_shape = [jax.ShapeDtypeStruct(*item) for item in made + kept]
    out_shape.append(jax.ShapeDtypeStruct((blocks, count * states, CB), BF16))
    out_shape.append(jax.ShapeDtypeStruct(*factors))
    scratch = [pltpu.VMEM(*item) for item in made] + [
        pltpu.VMEM(cube, F32),
        pltpu.VMEM(*factors),
        pltpu.VMEM(tall, F32),
        pltpu.VMEM(cube, F32),
        pltpu.VMEM(cube, F32),
        pltpu.VMEM(cube, F32),
        pltpu.VMEM(cube, F32),
        pltpu.VMEM((2 * blocks, width, CB), BF16),
        pltpu.VMEM((inner, width), BF16),
        pltpu.VMEM((count * states, CB), BF16),
        pltpu.VMEM((count * states, CB), BF16),
        pltpu.VMEM((count, width), BF16),
        pltpu.VMEM(cube, BF16),
        pltpu.VMEM(cube, F32),
        pltpu.VMEM(cube, F32),
        pltpu.VMEM((count, CB), jnp.int32),
        pltpu.VMEM((count * states, 128), F32),
        pltpu.VMEM((count // TB, 2 * TB, TB * states), BF16),
        pltpu.VMEM(cube, BF16),
        pltpu.SemaphoreType.DMA((2 * blocks,)),
        pltpu.SemaphoreType.DMA,
        pltpu.SemaphoreType.DMA((2,)),
        pltpu.SemaphoreType.DMA((blocks + 1,)),
        pltpu.SemaphoreType.DMA((len(kept), blocks)),
        pltpu.SemaphoreType.DMA((5,)),
    ]
    operands = [lengths, ids, rows, gain, in_w, conv_w, conv_b, sel_w, step_w, step_b, dlog, skip, out_w]
    in_specs = [smem(), smem(), vmem(), vmem(), hbm()] + [vmem()] * 7 + [hbm()]
    aliases = {}
    if earlier is not None:
        aliases = {len(operands) + item: item for item in range(len(out_shape))}
        operands += list(earlier)
        in_specs += [hbm()] * len(out_shape)
    return pl.pallas_call(
        partial(forward_kernel, number, earlier is not None),
        out_shape=out_shape,
        in_specs=in_specs,
        out_specs=[hbm()] * len(out_shape),
        scratch_shapes=scratch,
        input_output_aliases=aliases,
        compiler_params=pltpu.CompilerParams(vmem_limit_bytes=VMEM_LIMIT, has_side_effects=True),
        cost_estimate=LITTLE,
        name="layer_forward",
    )(*operands)


def gate_sends(ids, dz_v, dout_ref, sends, sem):
    part = dout_ref.shape[1] // PLANE
    copies = []
    for offset, target in enumerate(sends):
        place = jnp.bitwise_xor(ids[1], offset)
        columns = pl.ds(pl.multiple_of(place * part, part), part)
        copies.append(pltpu.make_async_copy(dz_v.at[place], target.at[:, pl.ds(0, CB)], sem.at[2 * offset]))
        copies.append(
            pltpu.make_async_copy(
                dout_ref.at[:, columns], target.at[:, pl.ds(CB, part)], sem.at[2 * offset + 1]
            )
        )
    return copies


def gate_kernel(number, ids, dout_ref, out_hbm, silu_hbm, slope_hbm, *rest):
    rest = rest[PLANE:]
    yb_hbm, *sends = rest[: 1 + PLANE]
    out_v, silu_v, slope_v, dg_v, dz_v, load_sem, keep_sem, send_sem = rest[1 + PLANE :]
    blocks, count, _ = silu_v.shape

    def body():
        loads = []
        for k in range(blocks):
            pairs = (
                (out_hbm.at[pl.ds(k * CB, CB), :], out_v.at[k]),
                (silu_hbm.at[k], silu_v.at[k]),
                (slope_hbm.at[k], slope_v.at[k]),
            )
            loads.append(
                [pltpu.make_async_copy(*pair, load_sem.at[item, k]) for item, pair in enumerate(pairs)]
            )
        for copies in loads:
            for copy in copies:
                copy.start()
        kept = []
        for k in range(blocks):
            for copy in loads[k]:
                copy.wait()
            dg_v[...] = mm_nt(dout_ref[...], out_v[k])

            def gate(step, _, k=k):
                at = pl.ds(pl.multiple_of(step * GATE_CHUNK, GATE_CHUNK), GATE_CHUNK)
                dg = dg_v[at, :]
                dz_v[k, at, :] = (dg * slope_v[k, at, :]).astype(BF16)
                silu_v[k, at, :] = dg * silu_v[k, at, :]
                return 0

            lax.fori_loop(0, count // GATE_CHUNK, gate, 0)
            copy = pltpu.make_async_copy(silu_v.at[k], yb_hbm.at[k], keep_sem.at[k])
            copy.start()
            kept.append(copy)
        for copy in gate_sends(ids, dz_v, dout_ref, sends, send_sem):
            copy.start()
            kept.append(copy)
        for copy in kept:
            copy.wait()

    pl.when(ids[0] == number)(body)


def backward_gate(number, ids, dout, weights, saved, earlier):
    out_w = weights[-1]
    silu, slope = saved[1:3]
    cube = silu.shape
    blocks, count, _ = cube
    shape = jax.ShapeDtypeStruct
    yb, *sends = pl.pallas_call(
        partial(gate_kernel, number),
        out_shape=[shape(cube, F32)] + [shape(earlier[0].shape, BF16)] * PLANE,
        in_specs=[smem(), vmem()] + [hbm()] * (3 + PLANE),
        out_specs=[hbm()] * (1 + PLANE),
        scratch_shapes=[
            pltpu.VMEM((blocks, CB, out_w.shape[1]), BF16),
            pltpu.VMEM(cube, F32),
            pltpu.VMEM(cube, F32),
            pltpu.VMEM((count, CB), F32),
            pltpu.VMEM(cube, BF16),
            pltpu.SemaphoreType.DMA((3, blocks)),
            pltpu.SemaphoreType.DMA((blocks,)),
            pltpu.SemaphoreType.DMA((2 * PLANE,)),
        ],
        input_output_aliases={5 + item: 1 + item for item in range(PLANE)},
        compiler_params=pltpu.CompilerParams(vmem_limit_bytes=VMEM_LIMIT, has_side_effects=True),
        cost_estimate=LITTLE,
        name="backward_gate",
    )(ids, dout, out_w, silu, slope, *earlier)
    return yb, sends


def backward_kernel(
    number,
    split,
    aliased,
    lengths,
    ids,
    rows_ref,
    dout_ref,
    gain_ref,
    in_hbm,
    cw_ref,
    cbias_ref,
    sel_ref,
    step_ref,
    dlog_ref,
    skip_ref,
    out_hbm,
    xi_hbm,
    z_hbm,
    y_hbm,
    delta_hbm,
    sig_hbm,
    xc_hbm,
    selt_ref,
    selo_ref,
    s_hbm,
    *rest,
):
    made = 2 + (1 if split else 2) * PLANE
    if split:
        yb_hbm, *gates = rest[: 1 + PLANE]
        rest = rest[1 + PLANE :]
    rest = rest[made if aliased else 0 :]
    da_hbm, dab_hbm, *sends = rest[:made]
    rest = rest[made:]
    (
        da_v,
        dab_v,
        dx_v,
        dz_v,
        pack_v,
        in_v,
        out_v,
        xi_v,
        z_v,
        y_v,
        delta_v,
        sig_v,
        s_v,
        dg_v,
        xc_v,
        xcb_v,
        dp_v,
        dxb_v,
        yb_v,
        ybb_v,
        dqb_v,
        pos_v,
        cb_v,
        bd_v,
        sb0_v,
        sb1_v,
        dw0_v,
        dw1_v,
        mb_v,
        mc_v,
        load_sem,
        s_sem,
        store_sem,
        gate_sem,
    ) = rest
    count, width = rows_ref.shape
    inner = cbias_ref.shape[1]
    blocks = inner // CB
    states = dlog_ref.shape[0]
    rank = step_ref.shape[0]
    picks = sel_ref.shape[0]
    taps = cw_ref.shape[0]
    at_step, at_decay = picks, picks + rank
    at_conv = at_decay + states
    at_cbias, at_sbias, at_skip, at_gain = (at_conv + taps + n for n in range(4))

    def body():
        def load(item, source, target, k):
            return pltpu.make_async_copy(source, target, load_sem.at[item, k])

        loads = []
        for k in range(blocks):
            part = pl.ds(k * CB, CB)
            first = [load(3, xc_hbm.at[k], xc_v.at[k], k), load(4, delta_hbm.at[k], delta_v.at[k], k)]
            if split:
                first.append(load(0, yb_hbm.at[k], yb_v.at[k], k))
            else:
                first.append(load(0, out_hbm.at[part, :], out_v.at[part, :], k))
                first.append(load(1, z_hbm.at[k], z_v.at[k, pl.ds(0, count), :], k))
                first.append(load(2, y_hbm.at[k], y_v.at[k], k))
            loads.append(first)
        gate_copies = []
        if split:
            for offset, gate in enumerate(gates):
                place = jnp.bitwise_xor(ids[1], offset)
                gate_copies.append(load(8, gate.at[:, pl.ds(0, CB)], dz_v.at[place], offset))
        sig_copy = load(5, sig_hbm, sig_v, 0)
        xi_copy = load(6, xi_hbm, xi_v, 0)
        in_copy = load(7, in_hbm, in_v, 0)

        def s_copy(k):
            return pltpu.make_async_copy(s_hbm.at[k], s_v.at[k % 2], s_sem.at[k % 2])

        for copies in loads:
            for copy in copies:
                copy.start()
        s_copy(0).start()
        s_copy(1).start()
        for copy in (sig_copy, xi_copy, *gate_copies, in_copy):
            copy.start()
        pos_v[:count, :] = places(lengths, count, CB)
        pos_v[count:, :] = jnp.zeros((8, CB), jnp.int32)
        spread_lanes(selt_ref[rank + states :, :], states, cb_v)
        spread_diagonal(selo_ref[:, rank : rank + states], states, bd_v)
        wide = TB * states
        ones = (
            iota((TB, wide), 1) // states == iota((TB, wide), 0)
        ).astype(BF16)
        mb_v[...] = jnp.zeros_like(mb_v)
        mc_v[...] = jnp.zeros_like(mc_v)

        for k in range(blocks):
            cols = slice(k * CB, (k + 1) * CB)
            for copy in loads[k]:
                copy.wait()
            if not split:
                dg_v[...] = mm_nt(dout_ref[...], out_v[cols, :])

            def gate(step, total, k=k, cols=cols):
                at = pl.ds(pl.multiple_of(step * CHUNK, CHUNK), CHUNK)
                xc = xc_v[k, at, :]
                xcb_v[k, at, :] = xc.astype(BF16)
                delta = delta_v[k, at, :]
                dp_v[k, at, :] = jnp.where(pos_v[at, :] == 0, FOREVER, delta)
                dxb_v[k, at, :] = (delta * xc).astype(BF16)
                if split:
                    ybar = yb_v[k, at, :]
                else:
                    dg = dg_v[at, :]
                    ybar = dg * z_v[k, at, :]
                    dz_v[k, at, :] = (dg * y_v[k, at, :]).astype(BF16)
                    yb_v[k, at, :] = ybar
                ybb_v[k, at, :] = ybar.astype(BF16)
                return total + fold8(ybar * xc)

            total = lax.fori_loop(0, count // CHUNK, gate, jnp.zeros((8, CB), F32))
            pack_v[at_skip : at_skip + 1, cols] = jnp.sum(total, axis=0, keepdims=True)
        r1_v, r2_v = y_v, z_v
        for k in range(blocks):
            cols = slice(k * CB, (k + 1) * CB)
            slot = k % 2
            s_copy(k).wait()
            natural = -jnp.exp(dlog_ref[:, cols])
            rate = natural * (1.0 / LN2)

            sb1_v[...] = jnp.zeros_like(sb1_v)
            dw1_v[...] = jnp.zeros_like(dw1_v)

            def gather(block, sb_v, dw_v, k=k):
                start = pl.multiple_of(block * TB, TB)
                rows_at = pl.ds(start, TB)
                both = mm(bd_v[block], sb_v[...])
                r1_v[k, rows_at, :] = both[:TB] + both[TB:]
                r2_v[k, rows_at, :] = mm(ones, dw_v[...]) * LN2
                mb_v[rows_at, :] += mm_nt(dxb_v[k, rows_at, :], sb_v[...])

            def walk(block, sb_v, dw_v, carry, total, k=k, slot=slot, rate=rate):
                start = pl.multiple_of(block * TB, TB)
                for token in reversed(range(TB)):
                    if token % 8 == 7:
                        at = pl.ds(pl.multiple_of(start + token - 7, 8), 8)
                        steps, ybars = dp_v[k, at, :], yb_v[k, at, :]
                    row = slice(token % 8, token % 8 + 1)
                    own = slice(token * states, (token + 1) * states)
                    here = pl.ds(pl.multiple_of((start + token) * states, states), states)
                    before = jnp.maximum(start + token - 1, 0)
                    there = pl.ds(pl.multiple_of(before * states, states), states)
                    power = steps[row] * rate
                    decay = jnp.exp2(power)
                    sbar = repeat_lanes(cb_v[here, :], CB // 128) * ybars[row] + carry
                    sb_v[own, :] = sbar.astype(BF16)
                    carry = sbar * decay
                    flow = carry * s_v[slot, there, :].astype(F32) * power
                    dw_v[own, :] = flow.astype(BF16)
                    total = total + flow
                return carry, total

            def read_in(block, k=k, slot=slot):
                start = pl.multiple_of(block * TB, TB)
                span = pl.ds(pl.multiple_of(start * states, wide), wide)
                rows_at = pl.ds(start, TB)
                mc_v[rows_at, :] += mm_nt(ybb_v[k, rows_at, :], s_v[slot, span, :])

            def scan(turn, state):
                carry, total = state
                upper = count // TB - 1 - 2 * turn
                gather(jnp.minimum(upper + 1, count // TB - 1), sb1_v, dw1_v)
                read_in(upper)
                carry, total = walk(upper, sb0_v, dw0_v, carry, total)
                gather(upper, sb0_v, dw0_v)
                read_in(upper - 1)
                return walk(upper - 1, sb1_v, dw1_v, carry, total)

            zero = jnp.zeros((states, CB), F32)
            _, total = lax.fori_loop(0, count // TB // 2, scan, (zero, zero))
            gather(0, sb1_v, dw1_v)
            pack_v[at_decay : at_decay + states, cols] = total * LN2
            if k + 2 < blocks:
                s_copy(k + 2).start()
        own = iota((count, wide), 0) % TB == iota((count, wide), 1) // states
        dsel = jnp.zeros((count, picks), F32)
        for values, base in ((mb_v, rank), (mc_v, rank + states)):
            pick = (iota((wide, picks), 0) % states + base == iota((wide, picks), 1)).astype(BF16)
            for piece in split_hi_lo(jnp.where(own, values[...], 0.0)):
                dsel = dsel + mm(piece, pick)
        dlbt = selt_ref[:rank, :].astype(BF16)
        sig_copy.wait()
        for k in range(blocks):
            cols = slice(k * CB, (k + 1) * CB)

            def steps(step, total, k=k, cols=cols):
                at = pl.ds(pl.multiple_of(step * CHUNK, CHUNK), CHUNK)
                r1 = r1_v[k, at, :]
                delta = delta_v[k, at, :]
                sig = sig_v[k, at, :]
                turned = pl.reciprocal(delta, approx=True)
                turned = turned * (2.0 - delta * turned)
                share = jnp.where(delta > 1e-30, sig * turned, 1.0)
                dq = r1 * xc_v[k, at, :] * sig + r2_v[k, at, :] * share
                dqb_v[k, at, :] = dq.astype(BF16)
                yb_v[k, at, :] = yb_v[k, at, :] * skip_ref[:, cols] + r1 * delta
                return total + fold8(dq)

            total = lax.fori_loop(0, count // CHUNK, steps, jnp.zeros((8, CB), F32))
            pack_v[at_sbias : at_sbias + 1, cols] = jnp.sum(total, axis=0, keepdims=True)
            place = (iota((rank, picks), 0) == iota((rank, picks), 1)).astype(BF16)
            ddl = mm_nt(dqb_v[k], step_ref[:, cols])
            for piece in split_hi_lo(ddl):
                dsel = dsel + mm(piece, place)
            pack_v[at_step : at_step + rank, cols] = mm(dlbt, dqb_v[k])
        dselb = dsel.astype(BF16)
        eye = (iota((count, count), 0) == iota((count, count), 1)).astype(BF16)
        dselt = lax.dot_general(
            dselb, eye, (((0,), (0,)), ((), ())), preferred_element_type=F32
        ).astype(BF16)
        xi_copy.wait()
        du = jnp.zeros((count, width), F32)
        for k in range(blocks):
            cols = slice(k * CB, (k + 1) * CB)
            pack_v[:picks, cols] = mm(dselt, xcb_v[k])
            dg_v[...] = mm(dselb, sel_ref[:, cols])
            dv_v = z_v
            dv_v[k, count:, :] = jnp.zeros((8, CB), F32)

            def pre(step, totals, k=k, cols=cols):
                start = pl.multiple_of(step * CHUNK, CHUNK)
                at = pl.ds(start, CHUNK)
                window = xi_v[k, pl.ds(start, CHUNK + 8), :]
                moved = conv_taps(window, pos_v[at, :], taps)
                value = conv_value(moved, cw_ref[:, cols], cbias_ref[:, cols])
                sv = jax.nn.sigmoid(value)
                dv = (yb_v[k, at, :] + dg_v[at, :]) * (sv * (1.0 + value * (1.0 - sv)))
                dv_v[k, at, :] = dv
                fresh = [fold8(dv)] + [fold8(dv * item) for item in moved]
                return tuple(total + item for total, item in zip(totals, fresh))

            zero = jnp.zeros((8, CB), F32)
            totals = lax.fori_loop(0, count // CHUNK, pre, (zero,) * (taps + 1))
            sums = [jnp.sum(total, axis=0, keepdims=True) for total in totals]
            pack_v[at_cbias : at_cbias + 1, cols] = sums[0]
            for delay in range(taps):
                row = at_conv + taps - 1 - delay
                pack_v[row : row + 1, cols] = sums[1 + delay]

            def turn_conv(step, _, k=k, cols=cols):
                start = pl.multiple_of(step * CHUNK, CHUNK)
                window = dv_v[k, pl.ds(start, CHUNK + 8), :]
                place = pos_v[pl.ds(start, CHUNK + 8), :]
                weight = cw_ref[:, cols]
                dxi = weight[taps - 1 : taps] * window[:CHUNK]
                for delay in range(1, taps):
                    masked = jnp.where(place >= delay, window, 0.0)
                    row = taps - 1 - delay
                    dxi = dxi + weight[row : row + 1] * masked[delay : delay + CHUNK]
                dx_v[k, pl.ds(start, CHUNK), :] = dxi.astype(BF16)
                return 0

            lax.fori_loop(0, count // CHUNK, turn_conv, 0)
        in_copy.wait()
        for copy in gate_copies:
            copy.wait()
        for k in range(blocks):
            du = du + mm_nt(dx_v[k, :count, :], in_v[:, k * CB : (k + 1) * CB])
            du = du + mm_nt(dz_v[k], in_v[:, inner + k * CB : inner + (k + 1) * CB])
        da_v[...] = du
        pack_v[at_gain:, :] = jnp.zeros((pack_v.shape[0] - at_gain, inner), F32)

        def unnorm(step, total):
            at = pl.ds(pl.multiple_of(step * CHUNK, CHUNK), CHUNK)
            a = rows_ref[at, :].astype(F32)
            scale = lax.rsqrt(jnp.mean(a * a, axis=-1, keepdims=True) + EPS)
            du = da_v[at, :]
            dn = du * gain_ref[...]
            lean = jnp.mean(a * dn, axis=-1, keepdims=True) * scale * scale * scale
            da = dout_ref[at, :].astype(F32) + dn * scale - a * lean
            da_v[at, :] = da
            dab_v[at, :] = da.astype(BF16)
            return total + fold8(du * a * scale)

        total = lax.fori_loop(0, count // CHUNK, unnorm, jnp.zeros((8, width), F32))
        pack_v[at_gain : at_gain + 1, :width] = jnp.sum(total, axis=0, keepdims=True)
        for k in range(blocks):
            dx_v[k, count:, :] = pack_v[:, k * CB : (k + 1) * CB].astype(BF16)
        stores = [(dab_v, dab_hbm), (da_v, da_hbm)]
        for offset, target in enumerate(sends[:PLANE]):
            stores.append((dx_v.at[jnp.bitwise_xor(ids[1], offset)], target))
        stores = [
            pltpu.make_async_copy(source, target, store_sem.at[item])
            for item, (source, target) in enumerate(stores)
        ]
        if not split:
            stores += gate_sends(ids, dz_v, dout_ref, sends[PLANE:], gate_sem)
        for copy in stores:
            copy.start()
        for copy in stores:
            copy.wait()

    pl.when(ids[0] == number)(body)


def backward(number, lengths, ids, rows, dout, weights, saved, gate, earlier, pack_rows):
    gain, in_w, conv_w, conv_b, sel_w, step_w, _, dlog, skip, out_w = weights
    count, width = rows.shape
    inner = conv_b.shape[1]
    blocks = inner // CB
    states = dlog.shape[0]
    cube = (blocks, count, CB)
    tall = (blocks, count + 8, CB)
    wide = TB * states
    shape = jax.ShapeDtypeStruct
    out_shape = [shape((count, width), F32), shape((count, width), BF16)]
    send = (count + pack_rows, CB)
    out_shape += [shape(send, BF16)] * PLANE
    if gate is None:
        out_shape += [shape((count, CB + width // PLANE), BF16)] * PLANE
    scratch = [
        pltpu.VMEM((count, width), F32),
        pltpu.VMEM((count, width), BF16),
        pltpu.VMEM((PLANE,) + send, BF16),
        pltpu.VMEM(cube, BF16),
        pltpu.VMEM((pack_rows, inner), F32),
        pltpu.VMEM(in_w.shape, BF16),
        pltpu.VMEM(out_w.shape if gate is None else (16, 128), BF16),
        pltpu.VMEM(tall, F32),
        pltpu.VMEM(tall, F32),
        pltpu.VMEM(cube, F32),
        pltpu.VMEM(cube, F32),
        pltpu.VMEM(cube, F32),
        pltpu.VMEM((2, count * states, CB), BF16),
        pltpu.VMEM((count, CB), F32),
        pltpu.VMEM(cube, F32),
        pltpu.VMEM(cube, BF16),
        pltpu.VMEM(cube, F32),
        pltpu.VMEM(cube, BF16),
        pltpu.VMEM(cube, F32),
        pltpu.VMEM(cube, BF16),
        pltpu.VMEM(cube, BF16),
        pltpu.VMEM((count + 8, CB), jnp.int32),
        pltpu.VMEM((count * states, 128), F32),
        pltpu.VMEM((count // TB, 2 * TB, wide), BF16),
        pltpu.VMEM((wide, CB), BF16),
        pltpu.VMEM((wide, CB), BF16),
        pltpu.VMEM((wide, CB), BF16),
        pltpu.VMEM((wide, CB), BF16),
        pltpu.VMEM((count, wide), F32),
        pltpu.VMEM((count, wide), F32),
        pltpu.SemaphoreType.DMA((9, max(blocks, PLANE))),
        pltpu.SemaphoreType.DMA((2,)),
        pltpu.SemaphoreType.DMA((2 + PLANE,)),
        pltpu.SemaphoreType.DMA((2 * PLANE,)),
    ]
    operands = [lengths, ids, rows, dout, gain, in_w, conv_w, conv_b, sel_w, step_w, dlog, skip, out_w]
    in_specs = [smem(), smem()] + [vmem()] * 3 + [hbm()] + [vmem()] * 6 + [hbm()]
    operands += list(saved)
    in_specs += [hbm()] * 6 + [vmem()] * 2 + [hbm()]
    if gate is not None:
        yb, gates = gate
        operands += [yb, *gates]
        in_specs += [hbm()] * (1 + PLANE)
    aliases = {}
    if earlier is not None:
        aliases = {len(operands) + item: item for item in range(len(out_shape))}
        operands += list(earlier)
        in_specs += [hbm()] * len(out_shape)
    return pl.pallas_call(
        partial(backward_kernel, number, gate is not None, earlier is not None),
        out_shape=out_shape,
        in_specs=in_specs,
        out_specs=[hbm()] * len(out_shape),
        scratch_shapes=scratch,
        input_output_aliases=aliases,
        compiler_params=pltpu.CompilerParams(vmem_limit_bytes=VMEM_LIMIT, has_side_effects=True),
        cost_estimate=LITTLE,
        name="layer_backward",
    )(*operands)


def bit_reverse(value, count):
    result = 0
    while count > 1:
        result, value, count = 2 * result + value % 2, value // 2, count // 2
    return result


def combine_kernel(early, ids, *refs):
    factors, sources = refs[:PLANE], refs[PLANE : 2 * PLANE]
    in_v, low_v, turned_v, moved_v, low_from, load_sem, moved_sem, sem = refs[-8:]
    line = sem.shape[0]
    kept, sent = refs[-10:-8]
    width = in_v.shape[0]
    rows = turned_v.shape[0]
    count = turned_v.shape[1] // PLANE
    step = 512
    loads = [
        [
            pltpu.make_async_copy(
                factor.at[pl.ds(start, step), :],
                turned_v.at[pl.ds(start, step), pl.ds(item * count, count)],
                load_sem.at[item, start // step],
            )
            for item, factor in enumerate(factors)
        ]
        for start in range(0, rows, step)
    ]
    fetches = []
    for item, source in enumerate(sources):
        target = moved_v.at[pl.ds(item * count, count), :]
        fetches.append(pltpu.make_async_copy(source.at[pl.ds(0, count), :], target, moved_sem.at[0, item]))
        if not early:
            extra = source.at[pl.ds(count, source.shape[0] - count), :]
            fetches.append(pltpu.make_async_copy(extra, low_from.at[item], moved_sem.at[1, item]))
    for copies in [fetches] + loads:
        for copy in copies:
            copy.start()
    for copy in fetches:
        copy.wait()
    for number, start in enumerate(range(0, rows, step)):
        for copy in loads[number]:
            copy.wait()
        for begin in range(start, start + step, 256):
            left = turned_v[begin : begin + 256, :]
            if start < width:
                in_v[begin : begin + 256, :] = mm(left, moved_v[:, :CB]).astype(BF16)
            else:
                low_v[begin - width : begin - width + 256, :] = mm(left, moved_v[:, CB:]).astype(BF16)
    if not early:
        total = low_from[0].astype(F32)
        for item in range(1, PLANE):
            total = total + low_from[item].astype(F32)
        low_v[...] = total.astype(BF16)
    copies = []
    half = width // line // 2
    parts = low_v.shape[1]
    folds = width // parts
    size = low_v.shape[0] // line // folds

    height = half + size

    def cut(source, start, size, target, item):
        part = source.at[pl.ds(pl.multiple_of(start, size), size), :]
        copies.append(pltpu.make_async_copy(part, target, sem.at[number, item]))

    for number in range(line):
        place = jnp.bitwise_xor(ids[2], bit_reverse(number, line))
        piece, base = (kept, number) if number < line // 2 else (sent, number - line // 2)
        base = base * height
        cut(in_v, 2 * place * half, half, piece.at[pl.ds(base, half), pl.ds(0, CB)], 0)
        cut(in_v, (2 * place + 1) * half, half, piece.at[pl.ds(base, half), pl.ds(CB, CB)], 1)
        for fold in range(folds):
            start = (place * folds + fold) * size if early else (fold * line + place) * size
            target = piece.at[pl.ds(base + half, size), pl.ds(fold * parts, parts)]
            cut(low_v, start, size, target, 2 + fold)
    for copy in copies:
        copy.start()
    for copy in copies:
        copy.wait()


def combine(early, ids, factors, moved, line, width, inner):
    wide, count = factors[0].shape
    tokens = PLANE * count
    if early:
        low, rows = (inner, width // PLANE), wide
    else:
        low, rows = (moved[0].shape[0] - count, CB), width
    piece = width // line // 2 + low[0] * low[1] // width // line
    return pl.pallas_call(
        partial(combine_kernel, early),
        out_shape=[jax.ShapeDtypeStruct((line // 2 * piece, width), BF16)] * 2,
        in_specs=[smem()] + [hbm()] * (2 * PLANE),
        out_specs=[hbm()] * 2,
        scratch_shapes=[
            pltpu.VMEM((width, CB), BF16),
            pltpu.VMEM(low, BF16),
            pltpu.VMEM((rows, tokens), BF16),
            pltpu.VMEM((tokens, moved[0].shape[1]), BF16),
            pltpu.VMEM((16, 128) if early else (PLANE,) + low, BF16),
            pltpu.SemaphoreType.DMA((PLANE, rows // 512)),
            pltpu.SemaphoreType.DMA((2, PLANE)),
            pltpu.SemaphoreType.DMA((line, 6)),
        ],
        compiler_params=pltpu.CompilerParams(vmem_limit_bytes=VMEM_LIMIT),
        cost_estimate=LITTLE,
        name="plane_sum",
    )(ids, *factors, *moved)


def place_kernel(early, first, last, line, places_of, small, ids, *refs):
    groups = [refs[5 * turn : 5 * turn + 5] for turn in range(len(places_of))]
    made = 2 if early else 1
    rest = refs[5 * len(places_of) + (0 if first else made) :]
    grads, rest = rest[:made], rest[made:]
    smalls = rest[:-6]
    hold, wide_in, wide_out, pack_v, load_sem, store_sem = rest[-6:]
    rows, high = hold.shape[1], wide_in.shape[1]
    half = high // 2
    low = rows - half
    jobs = []
    for group, places_here in zip(groups, places_of):
        cut = group[3].shape[0]
        for turn, at in enumerate(places_here):
            base = turn * rows
            for offset in range(PLANE - 1):
                jobs.append((offset, at, [(group[offset].at[pl.ds(base, rows), :], 0, rows)]))
            parts = []
            if base < cut:
                size = min(rows, cut - base)
                parts.append((group[3].at[pl.ds(base, size), :], 0, size))
            if base + rows > cut:
                begin = max(base, cut)
                parts.append((group[4].at[pl.ds(begin - cut, base + rows - begin), :], begin - base, base + rows - begin))
            jobs.append((PLANE - 1, at, parts))
    slots = hold.shape[0]

    def loads(number):
        return [
            pltpu.make_async_copy(
                source, hold.at[number % slots, pl.ds(begin, size), :], load_sem.at[number % slots, item]
            )
            for item, (source, begin, size) in enumerate(jobs[number][2])
        ]

    def stores(number):
        offset, at, _ = jobs[number]
        across, along = jnp.bitwise_xor(ids[1], offset), jnp.bitwise_xor(ids[2], at)
        slot = number % slots
        each = wide_in.shape[2]
        column = across * each + (PLANE * each if early else 0)
        copies = [
            pltpu.make_async_copy(
                wide_in.at[slot],
                grads[0].at[
                    pl.ds(pl.multiple_of(along * high, high), high), pl.ds(pl.multiple_of(column, each), each)
                ],
                store_sem.at[slot, 0],
            )
        ]
        if early:
            part = wide_out.shape[2] // PLANE
            columns = pl.ds(pl.multiple_of(across * part, part), part)
            for fold in range(PLANE):
                start = pl.multiple_of((along * PLANE + fold) * low, low)
                copies.append(
                    pltpu.make_async_copy(
                        wide_out.at[slot, :, pl.ds(fold * part, part)],
                        grads[1].at[pl.ds(start, low), columns],
                        store_sem.at[slot, 1 + fold],
                    )
                )
        return copies

    def put_pack(value, offset, at):
        across, along = jnp.bitwise_xor(ids[1], offset), jnp.bitwise_xor(ids[2], at)
        start = pl.multiple_of(along * low, low)
        pack_v[across, pl.ds(start, low), :] = value[:, :CB]
        pack_v[across, pl.ds(start + low * line, low), :] = value[:, CB:]

    for number in range(min(slots, len(jobs))):
        for copy in loads(number):
            copy.start()
    for number, (offset, at, _) in enumerate(jobs):
        slot = number % slots
        for copy in loads(number):
            copy.wait()
        if number >= slots:
            for copy in stores(number - slots):
                copy.wait()
        wide_in[slot, :half, :] = hold[slot, :half, :CB].astype(F32)
        wide_in[slot, half:, :] = hold[slot, :half, CB:].astype(F32)
        if early:
            wide_out[slot] = hold[slot, half:, :].astype(F32)
        else:
            put_pack(hold[slot, half:, :].astype(F32), offset, at)
        for copy in stores(number):
            copy.start()
        if number + slots < len(jobs):
            for copy in loads(number + slots):
                copy.start()
    if last:
        base = 0
        for size, ref in zip(small, smalls):
            for k in range(PLANE):
                cols = slice(k * CB, (k + 1) * CB)
                if cols.start < ref.shape[1]:
                    ref[:, cols] = pack_v[k, base : base + size, :]
            base += size
    for number in range(max(0, len(jobs) - slots), len(jobs)):
        for copy in stores(number):
            copy.wait()


def place_pieces(early, last, ids, groups, places_of, line, rows, width, inner, small, earlier):
    first = earlier is None
    high = width // line
    low = rows - high // 2
    shape = jax.ShapeDtypeStruct
    out_shape = [shape((width, 2 * inner), F32)]
    if early:
        out_shape.append(shape((inner, width), F32))
    aliased = len(out_shape)
    out_specs = [hbm()] * aliased
    operands = [ids]
    for group in groups:
        operands += group
    if last:
        out_shape += [shape((size, lanes), F32) for size, lanes in small]
        out_specs += [vmem()] * len(small)
    aliases = {}
    if not first:
        aliases = {len(operands) + item: item for item in range(aliased)}
        operands += list(earlier)
    chosen = tuple(tuple(item) for item in places_of)
    slots = 4
    return pl.pallas_call(
        partial(place_kernel, early, first, last, line, chosen, tuple(size for size, _ in small)),
        out_shape=out_shape,
        in_specs=[smem()] + [hbm()] * (len(operands) - 1),
        out_specs=out_specs,
        scratch_shapes=[
            pltpu.VMEM((slots, rows, width), BF16),
            pltpu.VMEM((slots, high, CB), F32),
            pltpu.VMEM((slots, low, width) if early else (8, 128), F32),
            pltpu.VMEM((8, 128) if early else (PLANE, 2 * low * line, CB), F32),
            pltpu.SemaphoreType.DMA((slots, 2)),
            pltpu.SemaphoreType.DMA((slots, 1 + PLANE)),
        ],
        input_output_aliases=aliases,
        compiler_params=pltpu.CompilerParams(vmem_limit_bytes=VMEM_LIMIT // 2),
        cost_estimate=LITTLE,
        name="place_gradients",
    )(*operands)


def trade(value, offset, clusters, sections=None):
    pairs = [(source, source ^ offset) for source in range(clusters)]
    if sections is None:
        return lax.ppermute(value, "dp", pairs)
    count, number = sections
    pairs = [(source * count + number, target * count + number) for source, target in pairs]
    return lax.ppermute(value, ("dp", "section"), pairs)


def trade_plane(values, clusters, sections=None):
    return [values[0]] + [trade(values[offset], offset, clusters, sections) for offset in range(1, PLANE)]


def tie(*values):
    return lax.optimization_barrier(values)


def line_sum_steps(kept, sent, line, clusters):
    bit = 1
    while True:
        (received,) = yield [trade(sent, bit * PLANE, clusters)]
        total = kept.astype(F32) + received.astype(F32)
        bit *= 2
        if bit == line:
            return total.astype(BF16)
        half = total.shape[0] // 2
        kept, sent = total[:half], total[half:].astype(BF16)


def forward_halves(rows, block, beside, above, clusters):
    cut = block.shape[0] // 2 if block.shape[0] > rows else rows // 32 * 16
    return [trade(above[:cut], 1, clusters), trade(beside[cut:], 2, clusters)]


def spread_steps(whole, line, clusters, apart):
    rows = whole.shape[0]
    blocks, places_of, groups, waiting = [whole], [[0]], [], None
    bit = line // 2
    while bit > 0:
        under_way = []
        if apart:
            under_way += [trade(blocks[-1], 1, clusters), trade(blocks[-1], 2, clusters)]
            if waiting is not None:
                under_way += forward_halves(rows, *waiting, clusters)
        under_way.append(trade(join(blocks), bit * PLANE, clusters))
        *under_way, fresh = yield under_way
        if apart:
            if waiting is not None:
                groups.append([*waiting, *under_way[2:]])
            waiting = [blocks[-1], *under_way[:2]]
        places_of.append([bit ^ at for places_here in places_of for at in places_here])
        blocks.append(fresh)
        bit //= 2
    if not apart:
        blocks, places_of = [join(blocks)], [[at for places_here in places_of for at in places_here]]
    under_way = [trade(blocks[-1], 1, clusters), trade(blocks[-1], 2, clusters)]
    if waiting is not None:
        under_way += forward_halves(rows, *waiting, clusters)
    under_way = yield under_way
    if waiting is not None:
        groups.append([*waiting, *under_way[2:]])
    waiting = [blocks[-1], *under_way[:2]]
    under_way = yield forward_halves(rows, *waiting, clusters)
    groups.append([*waiting, *under_way])
    return groups, places_of


def join(blocks):
    return blocks[0] if len(blocks) == 1 else jnp.concatenate(blocks, axis=0)


def chunk_steps(kept, sent, line, clusters, apart):
    whole = yield from line_sum_steps(kept, sent, line, clusters)
    groups, places_of = yield from spread_steps(whole, line, clusters, apart)
    return groups, places_of


def local(
    hidden_in,
    seq_lengths,
    norm_gain,
    in_proj,
    conv_weight,
    conv_bias,
    select_proj,
    step_proj,
    step_bias,
    decay_log,
    skip_gain,
    out_proj,
    cotangent,
):
    section = lax.axis_index("section")
    sections = lax.axis_size("section")
    cluster = lax.axis_index("dp")
    clusters = lax.axis_size("dp")
    line = clusters // PLANE
    ids = jnp.stack([section, cluster % PLANE, cluster // PLANE]).astype(jnp.int32)
    weights = (
        norm_gain,
        in_proj[0],
        conv_weight[0],
        conv_bias,
        select_proj[0],
        step_proj[0],
        step_bias,
        decay_log[0],
        skip_gain,
        out_proj[0],
    )
    width, inner = hidden_in.shape[1], conv_bias.shape[1]
    lanes = ((select_proj.shape[1], inner), (step_proj.shape[1], inner), (decay_log.shape[1], inner))
    small = lanes + ((conv_weight.shape[1], inner), (1, inner), (1, inner), (1, inner), (1, width))
    used = sum(rows for rows, _ in small)
    share = -(-used // (2 * line))
    pack_rows = 2 * line * (-(-share // 16) * 16)
    inputs, results = [hidden_in], None
    for number in range(sections):
        results = forward(number, seq_lengths, ids, inputs[number], weights, results)
        if number + 1 < sections:
            inputs.append(lax.ppermute(results[1], "section", [(number, number + 1)]))
    activations, _, selt, selo, *saved = results
    states_kept, factors = saved[6:]
    saved = [*saved[:6], selt, selo, states_kept]
    last = sections - 1
    factors = trade_plane([factors] * PLANE, clusters)
    dout, results = cotangent, None
    for number in reversed(range(1, sections)):
        results = backward(
            number, seq_lengths, ids, inputs[number], dout, weights, saved, None, results, pack_rows
        )
        dout = lax.ppermute(results[1], "section", [(number, number - 1)])
        if number == last:
            dout, factors = tie(dout, factors)
    yb, gates = backward_gate(0, ids, dout, weights, saved, results[2 + PLANE :])
    exchanged = trade_plane(gates, clusters)
    results = backward(
        0,
        seq_lengths,
        ids,
        inputs[0],
        dout,
        weights,
        saved,
        (yb, gates),
        results[: 2 + PLANE],
        pack_rows,
    )
    grads_rows, _, *moved = results
    moved, exchanged = tie(moved, exchanged)
    moved = trade_plane(moved, clusters)
    parts = combine(True, ids, factors, exchanged, line, width, inner)
    parts, moved = tie(parts, moved)
    early = chunk_steps(*parts, line, clusters, True)
    under_way = next(early)
    parts = combine(False, ids, factors, moved, line, width, inner)
    under_way, parts = tie(under_way, parts)
    late = chunk_steps(*parts, line, clusters, False)
    early_way, late_way = early.send(under_way), next(late)
    rows_early = width // line // 2 + inner // PLANE // line
    rows_late = width // line // 2 + pack_rows // line // 2
    sizes = (width, inner, small)
    groups = None
    while True:
        early_way, late_way = tie(early_way, late_way)
        if groups is None:
            try:
                early_way = early.send(early_way)
            except StopIteration as stop:
                groups, places_of = stop.value
                early_way = place_pieces(True, False, ids, groups, places_of, line, rows_early, *sizes, None)
        try:
            late_way = late.send(late_way)
        except StopIteration as stop:
            late_groups, late_places = stop.value
            break
    grad_in, grad_out = early_way
    grad_in, *smalls = place_pieces(
        False, True, ids, late_groups, late_places, line, rows_late, *sizes, [grad_in]
    )
    grad_sel, grad_step, grad_decay, grad_conv, grad_cbias, grad_sbias, grad_skip, grad_gain = smalls
    return (
        activations[None],
        grads_rows[None],
        grad_gain,
        grad_in[None],
        grad_conv[None],
        grad_cbias,
        grad_sel[None],
        grad_step[None],
        grad_sbias,
        grad_decay[None],
        grad_skip,
        grad_out[None],
    )


def solution(mesh):
    in_specs = (
        P("dp", None),
        P("dp", None),
        P("section", None),
        P("section", None, None),
        P("section", None, None),
        P("section", None),
        P("section", None, None),
        P("section", None, None),
        P("section", None),
        P("section", None, None),
        P("section", None),
        P("section", None, None),
        P("dp", None),
    )
    out_specs = (
        P("section", "dp", None),
        P("section", "dp", None),
        P("section", None),
        P("section", None, None),
        P("section", None, None),
        P("section", None),
        P("section", None, None),
        P("section", None, None),
        P("section", None),
        P("section", None, None),
        P("section", None),
        P("section", None, None),
    )
    return jax.shard_map(local, mesh=mesh, in_specs=in_specs, out_specs=out_specs, check_vma=False)
```

```python
from functools import partial
import math

import jax
import jax.numpy as jnp
from jax import lax
from jax.experimental import pallas as pl
from jax.experimental.pallas import tpu as pltpu
from jax.sharding import PartitionSpec as P

EPS = 1e-05
LN2 = math.log(2.0)
FOREVER = 1e30
TB = 16
CB = 512
GATE_CHUNK = 16
CHUNK = 128
WIDE_CHUNK = 256
F32 = jnp.float32
LITTLE = pl.CostEstimate(flops=10**6, bytes_accessed=10**4, transcendentals=0)
BF16 = jnp.bfloat16
PLANE = 4
VMEM_LIMIT = 60 * 1024 * 1024


def mm(a, b):
    return jnp.dot(a, b, preferred_element_type=F32)


def mm_nt(a, b):
    return lax.dot_general(a, b, (((1,), (1,)), ((), ())), preferred_element_type=F32)


def mm_tn(a, b):
    return lax.dot_general(a, b, (((0,), (0,)), ((), ())), preferred_element_type=F32)


def iota(shape, dim):
    return lax.broadcasted_iota(jnp.int32, shape, dim)


def split_hi_lo(value):
    hi = value.astype(BF16)
    return hi, (value - hi.astype(F32)).astype(BF16)


def softplus(value):
    small = jnp.exp(-jnp.abs(value))
    series = small * (1.0 - small * (0.5 - small * (1.0 / 3.0 - 0.25 * small)))
    return jnp.maximum(value, 0.0) + jnp.where(small < 2.0**-6, series, jnp.log(1.0 + small))


def places(lengths, rows, lanes):
    index = iota((rows, lanes), 0)
    begin = jnp.zeros((rows, lanes), jnp.int32)
    start = jnp.int32(0)
    for number in range(lengths.shape[1]):
        begin = jnp.where(index >= start, start, begin)
        start = start + lengths[0, number]
    return index - begin


def fold8(value):
    total = value[:8]
    for start in range(8, value.shape[0], 8):
        total = total + value[start : start + 8]
    return total


def spread_diagonal(columns, states, diag):
    count = columns.shape[0]
    wide = TB * states
    expand = (iota((states, wide), 1) % states == iota((states, wide), 0)).astype(BF16)
    own = iota((count, wide), 0) % TB == iota((count, wide), 1) // states
    for part, piece in enumerate(split_hi_lo(columns)):
        spread = jnp.where(own, mm(piece, expand), 0.0).astype(BF16)
        for block in range(count // TB):
            diag[block, part * TB : (part + 1) * TB, :] = spread[block * TB : (block + 1) * TB]


def spread_lanes(turned, states, wide):
    for token in range(turned.shape[1]):
        wide[token * states : (token + 1) * states, :] = jnp.broadcast_to(
            turned[:, token : token + 1], (states, wide.shape[1])
        )


def repeat_lanes(value, times):
    return jnp.concatenate([value] * times, axis=1)


def conv_taps(window, position, delays):
    taps = []
    for delay in range(delays):
        moved = window[8 - delay : 8 - delay + position.shape[0]]
        taps.append(moved if delay == 0 else jnp.where(position >= delay, moved, 0.0))
    return taps


def conv_value(taps, weight, bias):
    value = jnp.broadcast_to(bias, taps[0].shape)
    last = len(taps) - 1
    for delay, tap in enumerate(taps):
        value = value + weight[last - delay : last - delay + 1] * tap
    return value


def forward_kernel(
    number,
    aliased,
    lengths,
    ids,
    rows_ref,
    gain_ref,
    in_hbm,
    cw_ref,
    cbias_ref,
    sel_ref,
    step_ref,
    sbias_ref,
    dlog_ref,
    skip_ref,
    out_hbm,
    *rest,
):
    made = 12
    rest = rest[made if aliased else 0 :]
    out_hbm2, outb_hbm, selt_hbm, selo_hbm, *kept = rest[:10]
    s_hbm, factors = rest[10:12]
    rest = rest[12:]
    (
        result_v,
        low_v,
        selt_ref,
        selo_ref,
        sig_ref,
        turn_v,
        xi_ref,
        z_ref,
        y_ref,
        delta_ref,
        xc_v,
        in_v,
        out_v,
        s0_v,
        s1_v,
        u_v,
        xcb_v,
        dp_v,
        dx_v,
        pos_v,
        bb_v,
        cd_v,
        gb_v,
        in_sem,
        out_sem,
        s_sem,
        send_sem,
        keep_sem,
        last_sem,
    ) = rest
    count, width = rows_ref.shape
    inner = cbias_ref.shape[1]
    blocks = inner // CB
    states = dlog_ref.shape[0]
    rank = step_ref.shape[0]
    taps = cw_ref.shape[0]

    def body():
        started = []

        def keep(item, k):
            source = (xi_ref, z_ref, y_ref, delta_ref, sig_ref, xc_v)[item]
            copy = pltpu.make_async_copy(source.at[k], kept[item].at[k], keep_sem.at[item, k])
            copy.start()
            started.append(copy)

        in_copies = [
            pltpu.make_async_copy(in_hbm.at[:, pl.ds(k * CB, CB)], in_v.at[k], in_sem.at[k])
            for k in range(2 * blocks)
        ]
        out_copy = pltpu.make_async_copy(out_hbm, out_v, out_sem)
        for copy in in_copies:
            copy.start()
        out_copy.start()
        pos_v[...] = places(lengths, count, CB)

        def norm(step, _):
            at = pl.ds(pl.multiple_of(step * WIDE_CHUNK, WIDE_CHUNK), WIDE_CHUNK)
            a = rows_ref[at, :].astype(F32)
            scale = lax.rsqrt(jnp.mean(a * a, axis=-1, keepdims=True) + EPS)
            u_v[at, :] = (a * scale * gain_ref[...]).astype(BF16)
            return 0

        lax.fori_loop(0, count // WIDE_CHUNK, norm, 0)
        sel = jnp.zeros((count, sel_ref.shape[0]), F32)
        selt = jnp.zeros((sel_ref.shape[0], count), F32)
        for k in range(blocks):
            cols = slice(k * CB, (k + 1) * CB)
            in_copies[k].wait()
            xi_ref[k, 0:8, :] = jnp.zeros((8, CB), F32)
            xi_ref[k, 8:, :] = mm(u_v[...], in_v[k])

            def conv(step, _, k=k, cols=cols):
                start = pl.multiple_of(step * WIDE_CHUNK, WIDE_CHUNK)
                at = pl.ds(start, WIDE_CHUNK)
                window = xi_ref[k, pl.ds(start, WIDE_CHUNK + 8), :]
                value = conv_value(
                    conv_taps(window, pos_v[at, :], taps), cw_ref[:, cols], cbias_ref[:, cols]
                )
                xc = value * jax.nn.sigmoid(value)
                xc_v[k, at, :] = xc
                xcb_v[k, at, :] = xc.astype(BF16)
                return 0

            lax.fori_loop(0, count // WIDE_CHUNK, conv, 0)
            keep(0, k)
            keep(5, k)
            sel = sel + mm_nt(xcb_v[k], sel_ref[:, cols])
            selt = selt + mm_nt(sel_ref[:, cols], xcb_v[k])
        selo_ref[...] = sel
        selt_ref[...] = selt
        dlb = sel[:, :rank].astype(BF16)
        spread_lanes(selt_ref[rank : rank + states, :], states, bb_v)
        spread_diagonal(selo_ref[:, rank + states : rank + 2 * states], states, cd_v)
        for k in range(blocks):
            cols = slice(k * CB, (k + 1) * CB)
            delta_ref[k] = mm(dlb, step_ref[:, cols]) + sbias_ref[:, cols]

            def soften(step, _, k=k):
                at = pl.ds(pl.multiple_of(step * WIDE_CHUNK, WIDE_CHUNK), WIDE_CHUNK)
                q = delta_ref[k, at, :]
                delta = softplus(q)
                delta_ref[k, at, :] = delta
                sig_ref[k, at, :] = jax.nn.sigmoid(q)
                dp_v[k, at, :] = jnp.where(pos_v[at, :] == 0, FOREVER, delta)
                dx_v[k, at, :] = delta * xc_v[k, at, :]
                return 0

            lax.fori_loop(0, count // WIDE_CHUNK, soften, 0)
            keep(3, k)
            keep(4, k)
        for k in range(blocks):
            in_copies[blocks + k].wait()
            z_ref[k] = mm(u_v[...], in_v[blocks + k])

        s_v = (s0_v, s1_v)
        wide = TB * states

        def s_copy(k, slot):
            return pltpu.make_async_copy(s_v[slot], s_hbm.at[k], s_sem.at[slot])

        def read_out(k, block):
            start = pl.multiple_of(block * TB, TB)
            span = pl.ds(pl.multiple_of(start * states, wide), wide)
            both = mm(cd_v[block], s_v[k % 2][span, :])
            y_ref[k, pl.ds(start, TB), :] = both[:TB] + both[TB:]

        for k in range(blocks):
            cols = slice(k * CB, (k + 1) * CB)
            slot = k % 2
            if k >= 2:
                s_copy(k - 2, slot).wait()
            rate = -jnp.exp(dlog_ref[:, cols]) * (1.0 / LN2)

            def scan(block, state, k=k, slot=slot, rate=rate):
                start = pl.multiple_of(block * TB, TB)
                if k > 0:
                    read_out(k - 1, block)
                for token in range(TB):
                    if token % 8 == 0:
                        at = pl.ds(pl.multiple_of(start + token, 8), 8)
                        steps, drives = dp_v[k, at, :], dx_v[k, at, :]
                    row = slice(token % 8, token % 8 + 1)
                    here = pl.ds(pl.multiple_of((start + token) * states, states), states)
                    decay = jnp.exp2(steps[row] * rate)
                    state = decay * state + repeat_lanes(bb_v[here, :], CB // 128) * drives[row]
                    s_v[slot][here, :] = state.astype(BF16)
                return state

            lax.fori_loop(0, count // TB, scan, jnp.zeros((states, CB), F32))
            s_copy(k, slot).start()
        for block in range(count // TB):
            read_out(blocks - 1, block)
        for k in range(blocks):
            cols = slice(k * CB, (k + 1) * CB)

            def gate(step, _, k=k, cols=cols):
                at = pl.ds(pl.multiple_of(step * WIDE_CHUNK, WIDE_CHUNK), WIDE_CHUNK)
                z = z_ref[k, at, :]
                full = y_ref[k, at, :] + skip_ref[:, cols] * xc_v[k, at, :]
                sz = jax.nn.sigmoid(z)
                gated = z * sz
                gb_v[k, at, :] = (full * gated).astype(BF16)
                z_ref[k, at, :] = gated
                y_ref[k, at, :] = full * (sz * (1.0 + z * (1.0 - sz)))
                return 0

            lax.fori_loop(0, count // WIDE_CHUNK, gate, 0)
            keep(1, k)
            keep(2, k)
        copies = started
        for start in range(0, width, CB):
            turn_v[start : start + CB, :] = u_v[:, start : start + CB].astype(F32).T.astype(BF16)
        for k in range(blocks):
            turn_v[width + k * CB : width + (k + 1) * CB, :] = gb_v[k].astype(F32).T.astype(BF16)
        last = [(turn_v, factors), (selt_ref, selt_hbm), (selo_ref, selo_hbm)]
        out_copy.wait()
        result = rows_ref[...].astype(F32)
        for k in range(blocks):
            result = result + mm(gb_v[k], out_v[k * CB : (k + 1) * CB, :])
        result_v[...] = result
        low_v[...] = result.astype(BF16)
        last += [(low_v, outb_hbm), (result_v, out_hbm2)]
        last = [
            pltpu.make_async_copy(source, target, last_sem.at[item]) for item, (source, target) in enumerate(last)
        ]
        for copy in last:
            copy.start()
        for k in range(max(0, blocks - 2), blocks):
            s_copy(k, k % 2).wait()
        for copy in copies + last:
            copy.wait()

    pl.when(ids[0] == number)(body)


def vmem():
    return pl.BlockSpec(memory_space=pltpu.VMEM)


def smem():
    return pl.BlockSpec(memory_space=pltpu.SMEM)


def hbm():
    return pl.BlockSpec(memory_space=pl.ANY)


def forward(number, lengths, ids, rows, weights, earlier):
    gain, in_w, conv_w, conv_b, sel_w, step_w, step_b, dlog, skip, out_w = weights
    count, width = rows.shape
    inner = conv_b.shape[1]
    blocks = inner // CB
    states = dlog.shape[0]
    picks = sel_w.shape[0]
    cube = (blocks, count, CB)
    tall = (blocks, count + 8, CB)
    kept = [(tall, F32)] + [(cube, F32)] * 5
    made = [((count, width), F32), ((count, width), BF16), ((picks, count), F32), ((count, picks), F32)]
    factors = ((width + inner, count), BF16)
    out_shape = [jax.ShapeDtypeStruct(*item) for item in made + kept]
    out_shape.append(jax.ShapeDtypeStruct((blocks, count * states, CB), BF16))
    out_shape.append(jax.ShapeDtypeStruct(*factors))
    scratch = [pltpu.VMEM(*item) for item in made] + [
        pltpu.VMEM(cube, F32),
        pltpu.VMEM(*factors),
        pltpu.VMEM(tall, F32),
        pltpu.VMEM(cube, F32),
        pltpu.VMEM(cube, F32),
        pltpu.VMEM(cube, F32),
        pltpu.VMEM(cube, F32),
        pltpu.VMEM((2 * blocks, width, CB), BF16),
        pltpu.VMEM((inner, width), BF16),
        pltpu.VMEM((count * states, CB), BF16),
        pltpu.VMEM((count * states, CB), BF16),
        pltpu.VMEM((count, width), BF16),
        pltpu.VMEM(cube, BF16),
        pltpu.VMEM(cube, F32),
        pltpu.VMEM(cube, F32),
        pltpu.VMEM((count, CB), jnp.int32),
        pltpu.VMEM((count * states, 128), F32),
        pltpu.VMEM((count // TB, 2 * TB, TB * states), BF16),
        pltpu.VMEM(cube, BF16),
        pltpu.SemaphoreType.DMA((2 * blocks,)),
        pltpu.SemaphoreType.DMA,
        pltpu.SemaphoreType.DMA((2,)),
        pltpu.SemaphoreType.DMA((blocks + 1,)),
        pltpu.SemaphoreType.DMA((len(kept), blocks)),
        pltpu.SemaphoreType.DMA((5,)),
    ]
    operands = [lengths, ids, rows, gain, in_w, conv_w, conv_b, sel_w, step_w, step_b, dlog, skip, out_w]
    in_specs = [smem(), smem(), vmem(), vmem(), hbm()] + [vmem()] * 7 + [hbm()]
    aliases = {}
    if earlier is not None:
        aliases = {len(operands) + item: item for item in range(len(out_shape))}
        operands += list(earlier)
        in_specs += [hbm()] * len(out_shape)
    return pl.pallas_call(
        partial(forward_kernel, number, earlier is not None),
        out_shape=out_shape,
        in_specs=in_specs,
        out_specs=[hbm()] * len(out_shape),
        scratch_shapes=scratch,
        input_output_aliases=aliases,
        compiler_params=pltpu.CompilerParams(vmem_limit_bytes=VMEM_LIMIT, has_side_effects=True),
        cost_estimate=LITTLE,
        name="layer_forward",
    )(*operands)


def gate_sends(ids, dz_v, dout_ref, sends, sem):
    part = dout_ref.shape[1] // PLANE
    copies = []
    for offset, target in enumerate(sends):
        place = jnp.bitwise_xor(ids[1], offset)
        columns = pl.ds(pl.multiple_of(place * part, part), part)
        copies.append(pltpu.make_async_copy(dz_v.at[place], target.at[:, pl.ds(0, CB)], sem.at[2 * offset]))
        copies.append(
            pltpu.make_async_copy(
                dout_ref.at[:, columns], target.at[:, pl.ds(CB, part)], sem.at[2 * offset + 1]
            )
        )
    return copies


def gate_kernel(number, ids, dout_ref, out_hbm, silu_hbm, slope_hbm, *rest):
    rest = rest[PLANE:]
    yb_hbm, *sends = rest[: 1 + PLANE]
    out_v, silu_v, slope_v, dg_v, dz_v, load_sem, keep_sem, send_sem = rest[1 + PLANE :]
    blocks, count, _ = silu_v.shape

    def body():
        loads = []
        for k in range(blocks):
            pairs = (
                (out_hbm.at[pl.ds(k * CB, CB), :], out_v.at[k]),
                (silu_hbm.at[k], silu_v.at[k]),
                (slope_hbm.at[k], slope_v.at[k]),
            )
            loads.append(
                [pltpu.make_async_copy(*pair, load_sem.at[item, k]) for item, pair in enumerate(pairs)]
            )
        for copies in loads:
            for copy in copies:
                copy.start()
        kept = []
        for k in range(blocks):
            for copy in loads[k]:
                copy.wait()
            dg_v[...] = mm_nt(dout_ref[...], out_v[k])

            def gate(step, _, k=k):
                at = pl.ds(pl.multiple_of(step * GATE_CHUNK, GATE_CHUNK), GATE_CHUNK)
                dg = dg_v[at, :]
                dz_v[k, at, :] = (dg * slope_v[k, at, :]).astype(BF16)
                silu_v[k, at, :] = dg * silu_v[k, at, :]
                return 0

            lax.fori_loop(0, count // GATE_CHUNK, gate, 0)
            copy = pltpu.make_async_copy(silu_v.at[k], yb_hbm.at[k], keep_sem.at[k])
            copy.start()
            kept.append(copy)
        for copy in gate_sends(ids, dz_v, dout_ref, sends, send_sem):
            copy.start()
            kept.append(copy)
        for copy in kept:
            copy.wait()

    pl.when(ids[0] == number)(body)


def backward_gate(number, ids, dout, weights, saved, earlier):
    out_w = weights[-1]
    silu, slope = saved[1:3]
    cube = silu.shape
    blocks, count, _ = cube
    shape = jax.ShapeDtypeStruct
    yb, *sends = pl.pallas_call(
        partial(gate_kernel, number),
        out_shape=[shape(cube, F32)] + [shape(earlier[0].shape, BF16)] * PLANE,
        in_specs=[smem(), vmem()] + [hbm()] * (3 + PLANE),
        out_specs=[hbm()] * (1 + PLANE),
        scratch_shapes=[
            pltpu.VMEM((blocks, CB, out_w.shape[1]), BF16),
            pltpu.VMEM(cube, F32),
            pltpu.VMEM(cube, F32),
            pltpu.VMEM((count, CB), F32),
            pltpu.VMEM(cube, BF16),
            pltpu.SemaphoreType.DMA((3, blocks)),
            pltpu.SemaphoreType.DMA((blocks,)),
            pltpu.SemaphoreType.DMA((2 * PLANE,)),
        ],
        input_output_aliases={5 + item: 1 + item for item in range(PLANE)},
        compiler_params=pltpu.CompilerParams(vmem_limit_bytes=VMEM_LIMIT, has_side_effects=True),
        cost_estimate=LITTLE,
        name="backward_gate",
    )(ids, dout, out_w, silu, slope, *earlier)
    return yb, sends


def backward_kernel(
    number,
    split,
    aliased,
    lengths,
    ids,
    rows_ref,
    dout_ref,
    gain_ref,
    in_hbm,
    cw_ref,
    cbias_ref,
    sel_ref,
    step_ref,
    dlog_ref,
    skip_ref,
    out_hbm,
    xi_hbm,
    z_hbm,
    y_hbm,
    delta_hbm,
    sig_hbm,
    xc_hbm,
    selt_ref,
    selo_ref,
    s_hbm,
    *rest,
):
    chunk = 2 * CHUNK if split else CHUNK
    made = 2 + (1 if split else 2) * PLANE
    if split:
        yb_hbm, *gates = rest[: 1 + PLANE]
        rest = rest[1 + PLANE :]
    rest = rest[made if aliased else 0 :]
    da_hbm, dab_hbm, *sends = rest[:made]
    rest = rest[made:]
    (
        da_v,
        dab_v,
        dx_v,
        dz_v,
        pack_v,
        in_v,
        out_v,
        xi_v,
        z_v,
        y_v,
        delta_v,
        sig_v,
        s_v,
        dg_v,
        xc_v,
        xcb_v,
        dp_v,
        dxb_v,
        yb_v,
        ybb_v,
        dqb_v,
        pos_v,
        cb_v,
        bd_v,
        sb0_v,
        sb1_v,
        dw0_v,
        dw1_v,
        mb_v,
        mc_v,
        load_sem,
        s_sem,
        store_sem,
        gate_sem,
    ) = rest
    count, width = rows_ref.shape
    inner = cbias_ref.shape[1]
    blocks = inner // CB
    states = dlog_ref.shape[0]
    rank = step_ref.shape[0]
    picks = sel_ref.shape[0]
    taps = cw_ref.shape[0]
    at_step, at_decay = picks, picks + rank
    at_conv = at_decay + states
    at_cbias, at_sbias, at_skip, at_gain = (at_conv + taps + n for n in range(4))

    def body():
        def load(item, source, target, k):
            return pltpu.make_async_copy(source, target, load_sem.at[item, k])

        loads = []
        for k in range(blocks):
            part = pl.ds(k * CB, CB)
            first = [load(3, xc_hbm.at[k], xc_v.at[k], k), load(4, delta_hbm.at[k], delta_v.at[k], k)]
            if split:
                first.append(load(0, yb_hbm.at[k], yb_v.at[k], k))
            else:
                first.append(load(0, out_hbm.at[part, :], out_v.at[part, :], k))
                first.append(load(1, z_hbm.at[k], z_v.at[k, pl.ds(0, count), :], k))
                first.append(load(2, y_hbm.at[k], y_v.at[k], k))
            loads.append(first)
        gate_copies = []
        if split:
            for offset, gate in enumerate(gates):
                place = jnp.bitwise_xor(ids[1], offset)
                gate_copies.append(load(8, gate.at[:, pl.ds(0, CB)], dz_v.at[place], offset))
        sig_copy = load(5, sig_hbm, sig_v, 0)
        xi_copy = load(6, xi_hbm, xi_v, 0)
        in_copy = load(7, in_hbm, in_v, 0)

        def s_copy(k):
            return pltpu.make_async_copy(s_hbm.at[k], s_v.at[k % 2], s_sem.at[k % 2])

        for copies in loads:
            for copy in copies:
                copy.start()
        s_copy(0).start()
        s_copy(1).start()
        for copy in (sig_copy, xi_copy, *gate_copies, in_copy):
            copy.start()
        pos_v[:count, :] = places(lengths, count, CB)
        pos_v[count:, :] = jnp.zeros((8, CB), jnp.int32)
        spread_lanes(selt_ref[rank + states :, :], states, cb_v)
        spread_diagonal(selo_ref[:, rank : rank + states], states, bd_v)
        wide = TB * states
        ones = (
            iota((TB, wide), 1) // states == iota((TB, wide), 0)
        ).astype(BF16)
        mb_v[...] = jnp.zeros_like(mb_v)
        mc_v[...] = jnp.zeros_like(mc_v)

        for k in range(blocks):
            cols = slice(k * CB, (k + 1) * CB)
            for copy in loads[k]:
                copy.wait()
            if not split:
                dg_v[...] = mm_nt(dout_ref[...], out_v[cols, :])

            def gate(step, total, k=k, cols=cols):
                at = pl.ds(pl.multiple_of(step * chunk, chunk), chunk)
                xc = xc_v[k, at, :]
                xcb_v[k, at, :] = xc.astype(BF16)
                delta = delta_v[k, at, :]
                dp_v[k, at, :] = jnp.where(pos_v[at, :] == 0, FOREVER, delta)
                dxb_v[k, at, :] = (delta * xc).astype(BF16)
                if split:
                    ybar = yb_v[k, at, :]
                else:
                    dg = dg_v[at, :]
                    ybar = dg * z_v[k, at, :]
                    dz_v[k, at, :] = (dg * y_v[k, at, :]).astype(BF16)
                    yb_v[k, at, :] = ybar
                ybb_v[k, at, :] = ybar.astype(BF16)
                return total + fold8(ybar * xc)

            total = lax.fori_loop(0, count // chunk, gate, jnp.zeros((8, CB), F32))
            pack_v[at_skip : at_skip + 1, cols] = jnp.sum(total, axis=0, keepdims=True)
        r1_v, r2_v = y_v, z_v
        for k in range(blocks):
            cols = slice(k * CB, (k + 1) * CB)
            slot = k % 2
            s_copy(k).wait()
            natural = -jnp.exp(dlog_ref[:, cols])
            rate = natural * (1.0 / LN2)

            sb1_v[...] = jnp.zeros_like(sb1_v)
            dw1_v[...] = jnp.zeros_like(dw1_v)

            def gather(block, sb_v, dw_v, k=k):
                start = pl.multiple_of(block * TB, TB)
                rows_at = pl.ds(start, TB)
                both = mm(bd_v[block], sb_v[...])
                r1_v[k, rows_at, :] = both[:TB] + both[TB:]
                r2_v[k, rows_at, :] = mm(ones, dw_v[...]) * LN2
                mb_v[rows_at, :] += mm_nt(dxb_v[k, rows_at, :], sb_v[...])

            def walk(block, sb_v, dw_v, carry, total, k=k, slot=slot, rate=rate):
                start = pl.multiple_of(block * TB, TB)
                for token in reversed(range(TB)):
                    if token % 8 == 7:
                        at = pl.ds(pl.multiple_of(start + token - 7, 8), 8)
                        steps, ybars = dp_v[k, at, :], yb_v[k, at, :]
                    row = slice(token % 8, token % 8 + 1)
                    own = slice(token * states, (token + 1) * states)
                    here = pl.ds(pl.multiple_of((start + token) * states, states), states)
                    before = jnp.maximum(start + token - 1, 0)
                    there = pl.ds(pl.multiple_of(before * states, states), states)
                    power = steps[row] * rate
                    decay = jnp.exp2(power)
                    sbar = repeat_lanes(cb_v[here, :], CB // 128) * ybars[row] + carry
                    sb_v[own, :] = sbar.astype(BF16)
                    carry = sbar * decay
                    flow = carry * s_v[slot, there, :].astype(F32) * power
                    dw_v[own, :] = flow.astype(BF16)
                    total = total + flow
                return carry, total

            def read_in(block, k=k, slot=slot):
                start = pl.multiple_of(block * TB, TB)
                span = pl.ds(pl.multiple_of(start * states, wide), wide)
                rows_at = pl.ds(start, TB)
                mc_v[rows_at, :] += mm_nt(ybb_v[k, rows_at, :], s_v[slot, span, :])

            def scan(turn, state):
                carry, total = state
                upper = count // TB - 1 - 2 * turn
                gather(jnp.minimum(upper + 1, count // TB - 1), sb1_v, dw1_v)
                read_in(upper)
                carry, total = walk(upper, sb0_v, dw0_v, carry, total)
                gather(upper, sb0_v, dw0_v)
                read_in(upper - 1)
                return walk(upper - 1, sb1_v, dw1_v, carry, total)

            zero = jnp.zeros((states, CB), F32)
            _, total = lax.fori_loop(0, count // TB // 2, scan, (zero, zero))
            gather(0, sb1_v, dw1_v)
            pack_v[at_decay : at_decay + states, cols] = total * LN2
            if k + 2 < blocks:
                s_copy(k + 2).start()
        own = iota((count, wide), 0) % TB == iota((count, wide), 1) // states
        dsel = jnp.zeros((count, picks), F32)
        for values, base in ((mb_v, rank), (mc_v, rank + states)):
            pick = (iota((wide, picks), 0) % states + base == iota((wide, picks), 1)).astype(BF16)
            for piece in split_hi_lo(jnp.where(own, values[...], 0.0)):
                dsel = dsel + mm(piece, pick)
        dlbt = selt_ref[:rank, :].astype(BF16)
        sig_copy.wait()
        for k in range(blocks):
            cols = slice(k * CB, (k + 1) * CB)

            def steps(step, total, k=k, cols=cols):
                at = pl.ds(pl.multiple_of(step * chunk, chunk), chunk)
                r1 = r1_v[k, at, :]
                delta = delta_v[k, at, :]
                sig = sig_v[k, at, :]
                turned = pl.reciprocal(delta, approx=True)
                turned = turned * (2.0 - delta * turned)
                share = jnp.where(delta > 1e-30, sig * turned, 1.0)
                dq = r1 * xc_v[k, at, :] * sig + r2_v[k, at, :] * share
                dqb_v[k, at, :] = dq.astype(BF16)
                yb_v[k, at, :] = yb_v[k, at, :] * skip_ref[:, cols] + r1 * delta
                return total + fold8(dq)

            total = lax.fori_loop(0, count // chunk, steps, jnp.zeros((8, CB), F32))
            pack_v[at_sbias : at_sbias + 1, cols] = jnp.sum(total, axis=0, keepdims=True)
            place = (iota((rank, picks), 0) == iota((rank, picks), 1)).astype(BF16)
            ddl = mm_nt(dqb_v[k], step_ref[:, cols])
            for piece in split_hi_lo(ddl):
                dsel = dsel + mm(piece, place)
            pack_v[at_step : at_step + rank, cols] = mm(dlbt, dqb_v[k])
        dselb = dsel.astype(BF16)
        eye = (iota((count, count), 0) == iota((count, count), 1)).astype(BF16)
        dselt = lax.dot_general(
            dselb, eye, (((0,), (0,)), ((), ())), preferred_element_type=F32
        ).astype(BF16)
        xi_copy.wait()
        du = jnp.zeros((count, width), F32)
        for k in range(blocks):
            cols = slice(k * CB, (k + 1) * CB)
            pack_v[:picks, cols] = mm(dselt, xcb_v[k])
            dg_v[...] = mm(dselb, sel_ref[:, cols])
            dv_v = z_v
            dv_v[k, count:, :] = jnp.zeros((8, CB), F32)

            def pre(step, totals, k=k, cols=cols):
                start = pl.multiple_of(step * chunk, chunk)
                at = pl.ds(start, chunk)
                window = xi_v[k, pl.ds(start, chunk + 8), :]
                moved = conv_taps(window, pos_v[at, :], taps)
                value = conv_value(moved, cw_ref[:, cols], cbias_ref[:, cols])
                sv = jax.nn.sigmoid(value)
                dv = (yb_v[k, at, :] + dg_v[at, :]) * (sv * (1.0 + value * (1.0 - sv)))
                dv_v[k, at, :] = dv
                fresh = [fold8(dv)] + [fold8(dv * item) for item in moved]
                return tuple(total + item for total, item in zip(totals, fresh))

            zero = jnp.zeros((8, CB), F32)
            totals = lax.fori_loop(0, count // chunk, pre, (zero,) * (taps + 1))
            sums = [jnp.sum(total, axis=0, keepdims=True) for total in totals]
            pack_v[at_cbias : at_cbias + 1, cols] = sums[0]
            for delay in range(taps):
                row = at_conv + taps - 1 - delay
                pack_v[row : row + 1, cols] = sums[1 + delay]

            def turn_conv(step, _, k=k, cols=cols):
                start = pl.multiple_of(step * chunk, chunk)
                window = dv_v[k, pl.ds(start, chunk + 8), :]
                place = pos_v[pl.ds(start, chunk + 8), :]
                weight = cw_ref[:, cols]
                dxi = weight[taps - 1 : taps] * window[:chunk]
                for delay in range(1, taps):
                    masked = jnp.where(place >= delay, window, 0.0)
                    row = taps - 1 - delay
                    dxi = dxi + weight[row : row + 1] * masked[delay : delay + chunk]
                dx_v[k, pl.ds(start, chunk), :] = dxi.astype(BF16)
                return 0

            lax.fori_loop(0, count // chunk, turn_conv, 0)
        in_copy.wait()
        for copy in gate_copies:
            copy.wait()
        for k in range(blocks):
            du = du + mm_nt(dx_v[k, :count, :], in_v[:, k * CB : (k + 1) * CB])
            du = du + mm_nt(dz_v[k], in_v[:, inner + k * CB : inner + (k + 1) * CB])
        da_v[...] = du
        pack_v[at_gain:, :] = jnp.zeros((pack_v.shape[0] - at_gain, inner), F32)

        def unnorm(step, total):
            at = pl.ds(pl.multiple_of(step * chunk, chunk), chunk)
            a = rows_ref[at, :].astype(F32)
            scale = lax.rsqrt(jnp.mean(a * a, axis=-1, keepdims=True) + EPS)
            du = da_v[at, :]
            dn = du * gain_ref[...]
            lean = jnp.mean(a * dn, axis=-1, keepdims=True) * scale * scale * scale
            da = dout_ref[at, :].astype(F32) + dn * scale - a * lean
            da_v[at, :] = da
            dab_v[at, :] = da.astype(BF16)
            return total + fold8(du * a * scale)

        total = lax.fori_loop(0, count // chunk, unnorm, jnp.zeros((8, width), F32))
        pack_v[at_gain : at_gain + 1, :width] = jnp.sum(total, axis=0, keepdims=True)
        for k in range(blocks):
            dx_v[k, count:, :] = pack_v[:, k * CB : (k + 1) * CB].astype(BF16)
        stores = [(dab_v, dab_hbm), (da_v, da_hbm)]
        for offset, target in enumerate(sends[:PLANE]):
            stores.append((dx_v.at[jnp.bitwise_xor(ids[1], offset)], target))
        stores = [
            pltpu.make_async_copy(source, target, store_sem.at[item])
            for item, (source, target) in enumerate(stores)
        ]
        if not split:
            stores += gate_sends(ids, dz_v, dout_ref, sends[PLANE:], gate_sem)
        for copy in stores:
            copy.start()
        for copy in stores:
            copy.wait()

    pl.when(ids[0] == number)(body)


def backward(number, lengths, ids, rows, dout, weights, saved, gate, earlier, pack_rows):
    gain, in_w, conv_w, conv_b, sel_w, step_w, _, dlog, skip, out_w = weights
    count, width = rows.shape
    inner = conv_b.shape[1]
    blocks = inner // CB
    states = dlog.shape[0]
    cube = (blocks, count, CB)
    tall = (blocks, count + 8, CB)
    wide = TB * states
    shape = jax.ShapeDtypeStruct
    out_shape = [shape((count, width), F32), shape((count, width), BF16)]
    send = (count + pack_rows, CB)
    out_shape += [shape(send, BF16)] * PLANE
    if gate is None:
        out_shape += [shape((count, CB + width // PLANE), BF16)] * PLANE
    scratch = [
        pltpu.VMEM((count, width), F32),
        pltpu.VMEM((count, width), BF16),
        pltpu.VMEM((PLANE,) + send, BF16),
        pltpu.VMEM(cube, BF16),
        pltpu.VMEM((pack_rows, inner), F32),
        pltpu.VMEM(in_w.shape, BF16),
        pltpu.VMEM(out_w.shape if gate is None else (16, 128), BF16),
        pltpu.VMEM(tall, F32),
        pltpu.VMEM(tall, F32),
        pltpu.VMEM(cube, F32),
        pltpu.VMEM(cube, F32),
        pltpu.VMEM(cube, F32),
        pltpu.VMEM((2, count * states, CB), BF16),
        pltpu.VMEM((count, CB), F32),
        pltpu.VMEM(cube, F32),
        pltpu.VMEM(cube, BF16),
        pltpu.VMEM(cube, F32),
        pltpu.VMEM(cube, BF16),
        pltpu.VMEM(cube, F32),
        pltpu.VMEM(cube, BF16),
        pltpu.VMEM(cube, BF16),
        pltpu.VMEM((count + 8, CB), jnp.int32),
        pltpu.VMEM((count * states, 128), F32),
        pltpu.VMEM((count // TB, 2 * TB, wide), BF16),
        pltpu.VMEM((wide, CB), BF16),
        pltpu.VMEM((wide, CB), BF16),
        pltpu.VMEM((wide, CB), BF16),
        pltpu.VMEM((wide, CB), BF16),
        pltpu.VMEM((count, wide), F32),
        pltpu.VMEM((count, wide), F32),
        pltpu.SemaphoreType.DMA((9, max(blocks, PLANE))),
        pltpu.SemaphoreType.DMA((2,)),
        pltpu.SemaphoreType.DMA((2 + PLANE,)),
        pltpu.SemaphoreType.DMA((2 * PLANE,)),
    ]
    operands = [lengths, ids, rows, dout, gain, in_w, conv_w, conv_b, sel_w, step_w, dlog, skip, out_w]
    in_specs = [smem(), smem()] + [vmem()] * 3 + [hbm()] + [vmem()] * 6 + [hbm()]
    operands += list(saved)
    in_specs += [hbm()] * 6 + [vmem()] * 2 + [hbm()]
    if gate is not None:
        yb, gates = gate
        operands += [yb, *gates]
        in_specs += [hbm()] * (1 + PLANE)
    aliases = {}
    if earlier is not None:
        aliases = {len(operands) + item: item for item in range(len(out_shape))}
        operands += list(earlier)
        in_specs += [hbm()] * len(out_shape)
    return pl.pallas_call(
        partial(backward_kernel, number, gate is not None, earlier is not None),
        out_shape=out_shape,
        in_specs=in_specs,
        out_specs=[hbm()] * len(out_shape),
        scratch_shapes=scratch,
        input_output_aliases=aliases,
        compiler_params=pltpu.CompilerParams(vmem_limit_bytes=VMEM_LIMIT, has_side_effects=True),
        cost_estimate=LITTLE,
        name="layer_backward",
    )(*operands)


def bit_reverse(value, count):
    result = 0
    while count > 1:
        result, value, count = 2 * result + value % 2, value // 2, count // 2
    return result


def combine_kernel(early, ids, *refs):
    factors, sources = refs[:PLANE], refs[PLANE : 2 * PLANE]
    in_v, low_v, turned_v, moved_v, low_from, load_sem, moved_sem, sem = refs[-8:]
    line = sem.shape[0]
    kept, sent = refs[-10:-8]
    width = in_v.shape[0]
    rows = turned_v.shape[0]
    count = turned_v.shape[1] // PLANE
    step = 512
    loads = [
        [
            pltpu.make_async_copy(
                factor.at[pl.ds(start, step), :],
                turned_v.at[pl.ds(start, step), pl.ds(item * count, count)],
                load_sem.at[item, start // step],
            )
            for item, factor in enumerate(factors)
        ]
        for start in range(0, rows, step)
    ]
    fetches = []
    for item, source in enumerate(sources):
        target = moved_v.at[pl.ds(item * count, count), :]
        fetches.append(pltpu.make_async_copy(source.at[pl.ds(0, count), :], target, moved_sem.at[0, item]))
        if not early:
            extra = source.at[pl.ds(count, source.shape[0] - count), :]
            fetches.append(pltpu.make_async_copy(extra, low_from.at[item], moved_sem.at[1, item]))
    for copies in [fetches] + loads:
        for copy in copies:
            copy.start()
    for copy in fetches:
        copy.wait()
    for number, start in enumerate(range(0, rows, step)):
        for copy in loads[number]:
            copy.wait()
        for begin in range(start, start + step, 256):
            left = turned_v[begin : begin + 256, :]
            if start < width:
                in_v[begin : begin + 256, :] = mm(left, moved_v[:, :CB]).astype(BF16)
            else:
                low_v[begin - width : begin - width + 256, :] = mm(left, moved_v[:, CB:]).astype(BF16)
    if not early:
        total = low_from[0].astype(F32)
        for item in range(1, PLANE):
            total = total + low_from[item].astype(F32)
        low_v[...] = total.astype(BF16)
    copies = []
    half = width // line // 2
    parts = low_v.shape[1]
    folds = width // parts
    size = low_v.shape[0] // line // folds

    height = half + size

    def cut(source, start, size, target, item):
        part = source.at[pl.ds(pl.multiple_of(start, size), size), :]
        copies.append(pltpu.make_async_copy(part, target, sem.at[number, item]))

    for number in range(line):
        place = jnp.bitwise_xor(ids[2], bit_reverse(number, line))
        piece, base = (kept, number) if number < line // 2 else (sent, number - line // 2)
        base = base * height
        cut(in_v, 2 * place * half, half, piece.at[pl.ds(base, half), pl.ds(0, CB)], 0)
        cut(in_v, (2 * place + 1) * half, half, piece.at[pl.ds(base, half), pl.ds(CB, CB)], 1)
        for fold in range(folds):
            start = (place * folds + fold) * size if early else (fold * line + place) * size
            target = piece.at[pl.ds(base + half, size), pl.ds(fold * parts, parts)]
            cut(low_v, start, size, target, 2 + fold)
    for copy in copies:
        copy.start()
    for copy in copies:
        copy.wait()


def combine(early, ids, factors, moved, line, width, inner):
    wide, count = factors[0].shape
    tokens = PLANE * count
    if early:
        low, rows = (inner, width // PLANE), wide
    else:
        low, rows = (moved[0].shape[0] - count, CB), width
    piece = width // line // 2 + low[0] * low[1] // width // line
    return pl.pallas_call(
        partial(combine_kernel, early),
        out_shape=[jax.ShapeDtypeStruct((line // 2 * piece, width), BF16)] * 2,
        in_specs=[smem()] + [hbm()] * (2 * PLANE),
        out_specs=[hbm()] * 2,
        scratch_shapes=[
            pltpu.VMEM((width, CB), BF16),
            pltpu.VMEM(low, BF16),
            pltpu.VMEM((rows, tokens), BF16),
            pltpu.VMEM((tokens, moved[0].shape[1]), BF16),
            pltpu.VMEM((16, 128) if early else (PLANE,) + low, BF16),
            pltpu.SemaphoreType.DMA((PLANE, rows // 512)),
            pltpu.SemaphoreType.DMA((2, PLANE)),
            pltpu.SemaphoreType.DMA((line, 6)),
        ],
        compiler_params=pltpu.CompilerParams(vmem_limit_bytes=VMEM_LIMIT),
        cost_estimate=LITTLE,
        name="plane_sum",
    )(ids, *factors, *moved)


def place_kernel(early, first, last, line, places_of, small, ids, *refs):
    groups = [refs[5 * turn : 5 * turn + 5] for turn in range(len(places_of))]
    made = 2 if early else 1
    rest = refs[5 * len(places_of) + (0 if first else made) :]
    grads, rest = rest[:made], rest[made:]
    smalls = rest[:-6]
    hold, wide_in, wide_out, pack_v, load_sem, store_sem = rest[-6:]
    rows, high = hold.shape[1], wide_in.shape[1]
    half = high // 2
    low = rows - half
    jobs = []
    for group, places_here in zip(groups, places_of):
        cut = group[3].shape[0]
        for turn, at in enumerate(places_here):
            base = turn * rows
            for offset in range(PLANE - 1):
                jobs.append((offset, at, [(group[offset].at[pl.ds(base, rows), :], 0, rows)]))
            parts = []
            if base < cut:
                size = min(rows, cut - base)
                parts.append((group[3].at[pl.ds(base, size), :], 0, size))
            if base + rows > cut:
                begin = max(base, cut)
                parts.append((group[4].at[pl.ds(begin - cut, base + rows - begin), :], begin - base, base + rows - begin))
            jobs.append((PLANE - 1, at, parts))
    slots = hold.shape[0]

    def loads(number):
        return [
            pltpu.make_async_copy(
                source, hold.at[number % slots, pl.ds(begin, size), :], load_sem.at[number % slots, item]
            )
            for item, (source, begin, size) in enumerate(jobs[number][2])
        ]

    def stores(number):
        offset, at, _ = jobs[number]
        across, along = jnp.bitwise_xor(ids[1], offset), jnp.bitwise_xor(ids[2], at)
        slot = number % slots
        each = wide_in.shape[2]
        column = across * each + (PLANE * each if early else 0)
        copies = [
            pltpu.make_async_copy(
                wide_in.at[slot],
                grads[0].at[
                    pl.ds(pl.multiple_of(along * high, high), high), pl.ds(pl.multiple_of(column, each), each)
                ],
                store_sem.at[slot, 0],
            )
        ]
        if early:
            part = wide_out.shape[2] // PLANE
            columns = pl.ds(pl.multiple_of(across * part, part), part)
            for fold in range(PLANE):
                start = pl.multiple_of((along * PLANE + fold) * low, low)
                copies.append(
                    pltpu.make_async_copy(
                        wide_out.at[slot, :, pl.ds(fold * part, part)],
                        grads[1].at[pl.ds(start, low), columns],
                        store_sem.at[slot, 1 + fold],
                    )
                )
        return copies

    def put_pack(value, offset, at):
        across, along = jnp.bitwise_xor(ids[1], offset), jnp.bitwise_xor(ids[2], at)
        start = pl.multiple_of(along * low, low)
        pack_v[across, pl.ds(start, low), :] = value[:, :CB]
        pack_v[across, pl.ds(start + low * line, low), :] = value[:, CB:]

    for number in range(min(slots, len(jobs))):
        for copy in loads(number):
            copy.start()
    for number, (offset, at, _) in enumerate(jobs):
        slot = number % slots
        for copy in loads(number):
            copy.wait()
        if number >= slots:
            for copy in stores(number - slots):
                copy.wait()
        wide_in[slot, :half, :] = hold[slot, :half, :CB].astype(F32)
        wide_in[slot, half:, :] = hold[slot, :half, CB:].astype(F32)
        if early:
            wide_out[slot] = hold[slot, half:, :].astype(F32)
        else:
            put_pack(hold[slot, half:, :].astype(F32), offset, at)
        for copy in stores(number):
            copy.start()
        if number + slots < len(jobs):
            for copy in loads(number + slots):
                copy.start()
    if last:
        base = 0
        for size, ref in zip(small, smalls):
            for k in range(PLANE):
                cols = slice(k * CB, (k + 1) * CB)
                if cols.start < ref.shape[1]:
                    ref[:, cols] = pack_v[k, base : base + size, :]
            base += size
    for number in range(max(0, len(jobs) - slots), len(jobs)):
        for copy in stores(number):
            copy.wait()


def place_pieces(early, last, ids, groups, places_of, line, rows, width, inner, small, earlier):
    first = earlier is None
    high = width // line
    low = rows - high // 2
    shape = jax.ShapeDtypeStruct
    out_shape = [shape((width, 2 * inner), F32)]
    if early:
        out_shape.append(shape((inner, width), F32))
    aliased = len(out_shape)
    out_specs = [hbm()] * aliased
    operands = [ids]
    for group in groups:
        operands += group
    if last:
        out_shape += [shape((size, lanes), F32) for size, lanes in small]
        out_specs += [vmem()] * len(small)
    aliases = {}
    if not first:
        aliases = {len(operands) + item: item for item in range(aliased)}
        operands += list(earlier)
    chosen = tuple(tuple(item) for item in places_of)
    slots = 4
    return pl.pallas_call(
        partial(place_kernel, early, first, last, line, chosen, tuple(size for size, _ in small)),
        out_shape=out_shape,
        in_specs=[smem()] + [hbm()] * (len(operands) - 1),
        out_specs=out_specs,
        scratch_shapes=[
            pltpu.VMEM((slots, rows, width), BF16),
            pltpu.VMEM((slots, high, CB), F32),
            pltpu.VMEM((slots, low, width) if early else (8, 128), F32),
            pltpu.VMEM((8, 128) if early else (PLANE, 2 * low * line, CB), F32),
            pltpu.SemaphoreType.DMA((slots, 2)),
            pltpu.SemaphoreType.DMA((slots, 1 + PLANE)),
        ],
        input_output_aliases=aliases,
        compiler_params=pltpu.CompilerParams(vmem_limit_bytes=VMEM_LIMIT // 2),
        cost_estimate=LITTLE,
        name="place_gradients",
    )(*operands)


def trade(value, offset, clusters, sections=None):
    pairs = [(source, source ^ offset) for source in range(clusters)]
    if sections is None:
        return lax.ppermute(value, "dp", pairs)
    count, number = sections
    pairs = [(source * count + number, target * count + number) for source, target in pairs]
    return lax.ppermute(value, ("dp", "section"), pairs)


def trade_plane(values, clusters, sections=None):
    return [values[0]] + [trade(values[offset], offset, clusters, sections) for offset in range(1, PLANE)]


def tie(*values):
    return lax.optimization_barrier(values)


def line_sum_steps(kept, sent, line, clusters):
    bit = 1
    while True:
        (received,) = yield [trade(sent, bit * PLANE, clusters)]
        total = kept.astype(F32) + received.astype(F32)
        bit *= 2
        if bit == line:
            return total.astype(BF16)
        half = total.shape[0] // 2
        kept, sent = total[:half], total[half:].astype(BF16)


def forward_halves(rows, block, beside, above, clusters):
    cut = block.shape[0] // 2 if block.shape[0] > rows else rows // 32 * 16
    return [trade(above[:cut], 1, clusters), trade(beside[cut:], 2, clusters)]


def spread_steps(whole, line, clusters, apart):
    rows = whole.shape[0]
    blocks, places_of, groups, waiting = [whole], [[0]], [], None
    bit = line // 2
    while bit > 0:
        under_way = []
        if apart:
            under_way += [trade(blocks[-1], 1, clusters), trade(blocks[-1], 2, clusters)]
            if waiting is not None:
                under_way += forward_halves(rows, *waiting, clusters)
        under_way.append(trade(join(blocks), bit * PLANE, clusters))
        *under_way, fresh = yield under_way
        if apart:
            if waiting is not None:
                groups.append([*waiting, *under_way[2:]])
            waiting = [blocks[-1], *under_way[:2]]
        places_of.append([bit ^ at for places_here in places_of for at in places_here])
        blocks.append(fresh)
        bit //= 2
    if not apart:
        blocks, places_of = [join(blocks)], [[at for places_here in places_of for at in places_here]]
    under_way = [trade(blocks[-1], 1, clusters), trade(blocks[-1], 2, clusters)]
    if waiting is not None:
        under_way += forward_halves(rows, *waiting, clusters)
    under_way = yield under_way
    if waiting is not None:
        groups.append([*waiting, *under_way[2:]])
    waiting = [blocks[-1], *under_way[:2]]
    under_way = yield forward_halves(rows, *waiting, clusters)
    groups.append([*waiting, *under_way])
    return groups, places_of


def join(blocks):
    return blocks[0] if len(blocks) == 1 else jnp.concatenate(blocks, axis=0)


def chunk_steps(kept, sent, line, clusters, apart):
    whole = yield from line_sum_steps(kept, sent, line, clusters)
    groups, places_of = yield from spread_steps(whole, line, clusters, apart)
    return groups, places_of


def local(
    hidden_in,
    seq_lengths,
    norm_gain,
    in_proj,
    conv_weight,
    conv_bias,
    select_proj,
    step_proj,
    step_bias,
    decay_log,
    skip_gain,
    out_proj,
    cotangent,
):
    section = lax.axis_index("section")
    sections = lax.axis_size("section")
    cluster = lax.axis_index("dp")
    clusters = lax.axis_size("dp")
    line = clusters // PLANE
    ids = jnp.stack([section, cluster % PLANE, cluster // PLANE]).astype(jnp.int32)
    weights = (
        norm_gain,
        in_proj[0],
        conv_weight[0],
        conv_bias,
        select_proj[0],
        step_proj[0],
        step_bias,
        decay_log[0],
        skip_gain,
        out_proj[0],
    )
    width, inner = hidden_in.shape[1], conv_bias.shape[1]
    lanes = ((select_proj.shape[1], inner), (step_proj.shape[1], inner), (decay_log.shape[1], inner))
    small = lanes + ((conv_weight.shape[1], inner), (1, inner), (1, inner), (1, inner), (1, width))
    used = sum(rows for rows, _ in small)
    share = -(-used // (2 * line))
    pack_rows = 2 * line * (-(-share // 16) * 16)
    inputs, results = [hidden_in], None
    for number in range(sections):
        results = forward(number, seq_lengths, ids, inputs[number], weights, results)
        if number + 1 < sections:
            inputs.append(lax.ppermute(results[1], "section", [(number, number + 1)]))
    activations, _, selt, selo, *saved = results
    states_kept, factors = saved[6:]
    saved = [*saved[:6], selt, selo, states_kept]
    last = sections - 1
    factors = trade_plane([factors] * PLANE, clusters)
    dout, results = cotangent, None
    for number in reversed(range(1, sections)):
        results = backward(
            number, seq_lengths, ids, inputs[number], dout, weights, saved, None, results, pack_rows
        )
        dout = lax.ppermute(results[1], "section", [(number, number - 1)])
        if number == last:
            dout, factors = tie(dout, factors)
    yb, gates = backward_gate(0, ids, dout, weights, saved, results[2 + PLANE :])
    exchanged = trade_plane(gates, clusters)
    results = backward(
        0,
        seq_lengths,
        ids,
        inputs[0],
        dout,
        weights,
        saved,
        (yb, gates),
        results[: 2 + PLANE],
        pack_rows,
    )
    grads_rows, _, *moved = results
    moved, exchanged = tie(moved, exchanged)
    moved = trade_plane(moved, clusters)
    parts = combine(True, ids, factors, exchanged, line, width, inner)
    parts, moved = tie(parts, moved)
    early = chunk_steps(*parts, line, clusters, True)
    under_way = next(early)
    parts = combine(False, ids, factors, moved, line, width, inner)
    under_way, parts = tie(under_way, parts)
    late = chunk_steps(*parts, line, clusters, False)
    early_way, late_way = early.send(under_way), next(late)
    rows_early = width // line // 2 + inner // PLANE // line
    rows_late = width // line // 2 + pack_rows // line // 2
    sizes = (width, inner, small)
    groups = None
    while True:
        early_way, late_way = tie(early_way, late_way)
        if groups is None:
            try:
                early_way = early.send(early_way)
            except StopIteration as stop:
                groups, places_of = stop.value
                early_way = place_pieces(True, False, ids, groups, places_of, line, rows_early, *sizes, None)
        try:
            late_way = late.send(late_way)
        except StopIteration as stop:
            late_groups, late_places = stop.value
            break
    grad_in, grad_out = early_way
    grad_in, *smalls = place_pieces(
        False, True, ids, late_groups, late_places, line, rows_late, *sizes, [grad_in]
    )
    grad_sel, grad_step, grad_decay, grad_conv, grad_cbias, grad_sbias, grad_skip, grad_gain = smalls
    return (
        activations[None],
        grads_rows[None],
        grad_gain,
        grad_in[None],
        grad_conv[None],
        grad_cbias,
        grad_sel[None],
        grad_step[None],
        grad_sbias,
        grad_decay[None],
        grad_skip,
        grad_out[None],
    )


def solution(mesh):
    in_specs = (
        P("dp", None),
        P("dp", None),
        P("section", None),
        P("section", None, None),
        P("section", None, None),
        P("section", None),
        P("section", None, None),
        P("section", None, None),
        P("section", None),
        P("section", None, None),
        P("section", None),
        P("section", None, None),
        P("dp", None),
    )
    out_specs = (
        P("section", "dp", None),
        P("section", "dp", None),
        P("section", None),
        P("section", None, None),
        P("section", None, None),
        P("section", None),
        P("section", None, None),
        P("section", None, None),
        P("section", None),
        P("section", None, None),
        P("section", None),
        P("section", None, None),
    )
    return jax.shard_map(local, mesh=mesh, in_specs=in_specs, out_specs=out_specs, check_vma=False)
```
